32 devices in a mesh: lat: 16 (over z, x, core), lon: 2 (over y).
Axes of the slice: x: 2, y: 2, z: 4, core: 2. Of those that a mesh axis runs over, the one named last changes fastest.
Arguments:
- x_tiles: bfloat16 [2, 64, 77, 256], P('lon', 'lat'), may hold values from -6 to 6
- tile_pos: int32 [2, 64], P('lon', 'lat'), may hold values from 0 to 511, as said below
- valid_rows: int32 [2, 64], P('lon', 'lat'), may hold values from 1 to 16
- stem_w: bfloat16 [77, 200], replicated, may hold values from -0.625 to 0.625
- dw_kernel: float32 [200, 49], replicated, may hold values from -0.875 to 0.875
- norm_gain: float32 [200], replicated, may hold values from 0.1 to 1.9
- w_in: bfloat16 [200, 800], replicated, may hold values from -0.4375 to 0.4375
- w_out: bfloat16 [800, 200], replicated, may hold values from -0.21875 to 0.21875
- cotangent: bfloat16 [2, 64, 200, 256], P('lon', 'lat'), may hold values from -3072 to 3072
Outputs:
- out_tiles: bfloat16 [2, 64, 200, 256], P('lon', 'lat')
- grad_w_in: float32 [200, 800], replicated
- grad_w_out: float32 [800, 200], replicated
- grad_kernel: float32 [200, 49], replicated
- grad_gain: float32 [200], replicated
The draws below stay inside these ranges and needn't reach their ends.
Inputs may be any that keep to these rules, and one draw needn't show every extreme that they name: `tile_pos`: in each sector the places are distinct; in the order of place, the r-th active tile of a sector is held by lat index r % 16. At most 2 tiles of one device lie in one band block of 32 tiles, and this is reached; some band block is fully active in every sector.
All inputs are finite; a program needn't handle non-finite values.
Results may differ from the reference program's by a relative error of at most 0.0075.
Values may be sent and summed in bfloat16 or wider, within the bound.
A program may use at most 128 MiB of HBM per device.

```python
import jax
import jax.numpy as jnp
from jax import lax

C = 200
CIN = 77
HID = 800
KW = 7
TS = 16
BH = 64
BW = 128
A_DEV = 4
TT = 256
K_TILES = 32
ACT = 64
N_LAT = 16
N_LON = 2


def draw_tile_pos(key, part):
    tiles_all = K_TILES * N_LAT
    picked = A_DEV * N_LAT

    def one_sector(sector_key):
        base_key, band_key, full_key = jax.random.split(sector_key, 3)
        tile_index = jnp.arange(tiles_all, dtype=jnp.int32)
        band_of = tile_index // K_TILES
        base_score = jax.random.randint(base_key, (tiles_all,), 0, 4096)
        band_bias = jax.random.randint(band_key, (N_LAT,), 0, 8192)
        full_band = jax.random.randint(full_key, (), 0, N_LAT)
        forced = jnp.where((band_of == full_band) | (tile_index == 0) | (tile_index == tiles_all - 1), 16384, 0)
        score_all = (base_score + band_bias[band_of] + forced) * tiles_all + tile_index
        chosen = jnp.sort(lax.top_k(score_all, picked)[1])
        return chosen.reshape(A_DEV, N_LAT).T.reshape(picked).astype(jnp.int32)
    sector_keys = jax.random.split(key, N_LON)
    return jax.vmap(one_sector)(sector_keys)


def draw_valid_rows(key, part):
    drawn = jax.random.randint(key, (N_LON, A_DEV * N_LAT), 1, TS + 1)
    drawn = drawn.at[:, 0].set(TS)
    return drawn.at[:, 1].set(1).astype(jnp.int32)


def block_scale(stream_key, dims, shards, least, top_value):
    factor_of = 1.0
    for position, shards_of in shards:
        heights = jax.random.uniform(jax.random.fold_in(jax.random.fold_in(stream_key, 6), position), (shards_of,), jnp.float32, least / len(shards), top_value / len(shards))
        factor_of = factor_of * jnp.repeat(jnp.exp(heights), dims[position] // shards_of).reshape((-1,) + (1,) * (len(dims) - 1 - position))
    return factor_of


def bell_draw(stream_key, shape, deviation, most, pieces=(), held_as=jnp.bfloat16):
    entries = jax.random.normal(stream_key, shape, jnp.float32) * deviation
    if len(pieces) > 0:
        entries = block_scale(stream_key, shape, pieces, -0.22, 0.18) * entries
    return jnp.clip(entries, min=-most, max=most).astype(held_as)


def setup_inputs(seed: int = 0) -> dict:
    key_list = jax.random.split(jax.random.key(seed), 10)
    x_tiles = bell_draw(key_list[0], (N_LON, ACT, CIN, TT), 1.0, 6.0, ((0, 2), (1, 16)))
    tile_pos = draw_tile_pos(jax.random.fold_in(key_list[9], 71), 0)
    valid_rows = draw_valid_rows(jax.random.fold_in(key_list[9], 71), 0)
    stem_w = bell_draw(key_list[3], (CIN, C), CIN ** -0.5, 0.625)
    dw_kernel = bell_draw(key_list[4], (C, KW * KW), (KW * KW) ** -0.5, 0.875, (), jnp.float32)
    norm_gain = jnp.clip(1.0 + 0.18 * jax.random.normal(key_list[5], (C,), jnp.float32), 0.1, 1.9)
    w_in = bell_draw(key_list[6], (C, HID), C ** -0.5, 0.4375)
    w_out = bell_draw(key_list[7], (HID, C), HID ** -0.5, 0.21875)
    cotangent = bell_draw(key_list[8], (N_LON, ACT, C, TT), 512.0, 3072.0, ((0, 2), (1, 16)))
    return {"x_tiles": x_tiles, "tile_pos": tile_pos, "valid_rows": valid_rows, "stem_w": stem_w, "dw_kernel": dw_kernel, "norm_gain": norm_gain, "w_in": w_in, "w_out": w_out, "cotangent": cotangent}


def gelu_tanh(value):
    return jax.nn.gelu(value, approximate=True)

def to_grid(grid_tiles):
    chan = grid_tiles.shape[2]
    shaped = grid_tiles.reshape(N_LON, N_LAT, BH // TS, BW // TS, chan, TS, TS)
    return shaped.transpose(4, 1, 2, 5, 0, 3, 6).reshape(chan, BH * N_LAT, BW * N_LON)

def from_grid(grid):
    chan = grid.shape[0]
    shaped = grid.reshape(chan, N_LAT, BH // TS, TS, N_LON, BW // TS, TS)
    return shaped.transpose(4, 1, 2, 5, 0, 3, 6).reshape(N_LON, N_LAT * K_TILES, chan, TS * TS)

def place_tiles(values, tile_pos):
    sector_ids = jnp.arange(N_LON, dtype=jnp.int32)[:, None]
    empty = jnp.zeros((N_LON, N_LAT * K_TILES, values.shape[2], TS * TS), values.dtype)
    return to_grid(empty.at[sector_ids, tile_pos].set(values))

def pick_tiles(grid, tile_pos):
    sector_ids = jnp.arange(N_LON, dtype=jnp.int32)[:, None]
    return from_grid(grid)[sector_ids, tile_pos]

def band_rows(lat_pad, band_index):
    reach = KW // 2
    start = (band_index * BH).astype(jnp.int32)
    rows = lax.dynamic_slice_in_dim(lat_pad, start, BH + 2 * reach, axis=1)
    return jnp.concatenate([rows[:, :, -reach:], rows, rows[:, :, :reach]], axis=2)

def band_norm(padded, dw_kernel):
    width = padded.shape[2] - 2 * (KW // 2)
    conv_out = jnp.zeros((padded.shape[0], BH, width), jnp.float32)
    for tap_index in range(KW * KW):
        row_off = tap_index // KW
        col_off = tap_index % KW
        conv_out = conv_out + dw_kernel[:, tap_index][:, None, None] * padded[:, row_off:row_off + BH, col_off:col_off + width].astype(jnp.float32)
    centred = conv_out - lax.optimization_barrier(jnp.mean(conv_out, axis=0, keepdims=True))
    inv_std = lax.rsqrt(lax.optimization_barrier(jnp.mean(centred * centred, axis=0, keepdims=True)) + 1e-06)
    return (centred * inv_std, inv_std)

def stack_bands(banded):
    chan = banded.shape[1]
    return banded.transpose(1, 0, 2, 3).reshape(chan, N_LAT * BH, banded.shape[3])

def reference(x_tiles, tile_pos, valid_rows, stem_w, dw_kernel, norm_gain, w_in, w_out, cotangent):
    f32 = jnp.float32
    bf16 = jnp.bfloat16
    reach = KW // 2
    cell_rows = jnp.arange(TS * TS, dtype=jnp.int32) // TS
    ocean_mask = (cell_rows[None, None, :] < valid_rows[:, :, None]).astype(f32)
    stem_tiles = (jnp.einsum('kc,sakp->sacp', stem_w.astype(f32), x_tiles.astype(f32)) * ocean_mask[:, :, None, :]).astype(bf16)
    band_grid = place_tiles(stem_tiles, tile_pos)
    lat_pad = jnp.pad(band_grid, ((0, 0), (reach, reach), (0, 0)))
    band_ids = jnp.arange(N_LAT, dtype=jnp.int32)

    def forward_band(band_index):
        unit, inv_std = band_norm(band_rows(lat_pad, band_index), dw_kernel)
        return (unit * norm_gain[:, None, None]).astype(bf16)
    normed = stack_bands(lax.map(forward_band, band_ids))
    features = pick_tiles(normed, tile_pos)

    def sector_work(items):
        feats, stems, upstream, mask_s = items
        preact = jnp.einsum('ch,acp->ahp', w_in.astype(f32), feats.astype(f32))
        hidden = gelu_tanh(preact).astype(bf16)
        branch = jnp.einsum('hc,ahp->acp', w_out.astype(f32), hidden.astype(f32))
        result = (mask_s[:, None, :] * (stems.astype(f32) + branch)).astype(bf16)
        masked_grad = (upstream.astype(f32) * mask_s[:, None, :]).astype(bf16)
        grad_hidden = jnp.einsum('hc,acp->ahp', w_out.astype(f32), masked_grad.astype(f32))
        grad_preact = jax.vjp(gelu_tanh, preact)[1](grad_hidden)[0].astype(bf16)
        grad_feats = jnp.einsum('ch,ahp->acp', w_in.astype(f32), grad_preact.astype(f32)).astype(bf16)
        part_in = jnp.einsum('acp,ahp->ch', feats.astype(f32), grad_preact.astype(f32))
        part_out = jnp.einsum('ahp,acp->hc', hidden.astype(f32), masked_grad.astype(f32))
        return (result, grad_feats, part_in, part_out)
    out_tiles, grad_features, parts_in, parts_out = lax.map(sector_work, (features, stem_tiles, cotangent, ocean_mask))
    grad_grid = place_tiles(grad_features, tile_pos)

    def backward_band(band_index):
        padded = band_rows(lat_pad, band_index)
        unit, inv_std = band_norm(padded, dw_kernel)
        start = (band_index * BH).astype(jnp.int32)
        grad_band = lax.dynamic_slice_in_dim(grad_grid, start, BH, axis=1).astype(f32)
        scaled = grad_band * norm_gain[:, None, None]
        grad_conv = inv_std * (scaled - lax.optimization_barrier(jnp.mean(scaled, axis=0, keepdims=True)) - unit * lax.optimization_barrier(jnp.mean(scaled * unit, axis=0, keepdims=True)))
        width = grad_band.shape[2]
        kernel_terms = []
        for tap_index in range(KW * KW):
            row_off = tap_index // KW
            col_off = tap_index % KW
            kernel_terms.append(lax.optimization_barrier(jnp.sum(grad_conv * padded[:, row_off:row_off + BH, col_off:col_off + width].astype(f32), axis=(1, 2))))
        return (jnp.stack(kernel_terms, axis=1), lax.optimization_barrier(jnp.sum(grad_band * unit, axis=(1, 2))))
    kernel_parts, gain_parts = lax.map(backward_band, band_ids)
    cell_total = TS * jnp.sum(valid_rows.astype(f32))
    grad_kernel = lax.optimization_barrier(jnp.sum(kernel_parts, axis=0)) / cell_total
    grad_gain = lax.optimization_barrier(jnp.sum(gain_parts, axis=0)) / cell_total
    grad_w_in = lax.optimization_barrier(jnp.sum(parts_in, axis=0)) / cell_total
    grad_w_out = lax.optimization_barrier(jnp.sum(parts_out, axis=0)) / cell_total
    return (out_tiles, grad_w_in, grad_w_out, grad_kernel, grad_gain)
```

```python
import functools

import jax
import jax.numpy as jnp
import numpy as np
from jax import lax
from jax.experimental import pallas as pl
from jax.experimental.pallas import tpu as pltpu
from jax.sharding import PartitionSpec as P

TS = 16
CELLS = TS * TS
KW = 7
REACH = KW // 2
TCOLS = 8
EDGE = 160
PR = TS + 2 * REACH
PC = 24
CINP = 80
KROWS = CELLS + 8 * EDGE
OFFSETS = ((-1, -1), (-1, 0), (-1, 1), (0, -1), (0, 1), (1, -1), (1, 0), (1, 1))
VMEM_LIMIT = 56 * 1024 * 1024


def edge_index():
    table = -np.ones((TS, TS), np.int64)
    count = 0
    for y in range(TS):
        for x in range(TS):
            if min(y, x) < REACH or max(y, x) >= TS - REACH:
                table[y, x] = count
                count += 1
    return table


def edge_pick(tile_count):
    table = edge_index()
    pick = np.zeros((tile_count, CELLS, tile_count * EDGE), np.float32)
    for y in range(TS):
        for x in range(TS):
            if table[y, x] >= 0:
                for a in range(tile_count):
                    pick[a, y * TS + x, a * EDGE + table[y, x]] = 1
    return pick


def halo_pick():
    table = edge_index()
    pick = np.zeros((KROWS, PR * PC), np.float32)
    for py in range(PR):
        for px in range(PR):
            y, x = py - REACH, px - REACH
            dy, dx = y // TS, x // TS
            cell = py * PC + px
            if (dy, dx) == (0, 0):
                pick[y * TS + x, cell] = 1
            else:
                n = OFFSETS.index((dy, dx))
                pick[CELLS + n * EDGE + table[y % TS, x % TS], cell] = 1
    return pick


def pack_kernel(places, rows, x_ref, pick_ref, out_ref, held):
    tile_count = x_ref.shape[0]
    lanes = tile_count * EDGE
    cell_row = lax.broadcasted_iota(jnp.int32, (1, CELLS), 1) // TS
    total = jnp.zeros((x_ref.shape[1], lanes), jnp.float32)
    for a in range(tile_count):
        keep = (cell_row < rows[a]).astype(jnp.float32)
        tile = (x_ref[a].astype(jnp.float32) * keep).astype(jnp.bfloat16)
        total += jnp.dot(tile, pick_ref[a], preferred_element_type=jnp.float32)
    held[...] = jnp.zeros_like(held)
    held[0 : x_ref.shape[1], :] = total
    owner = lax.broadcasted_iota(jnp.int32, (1, lanes), 1) // EDGE
    high = jnp.zeros((1, lanes), jnp.int32)
    low = jnp.zeros((1, lanes), jnp.int32)
    ocean = jnp.zeros((1, lanes), jnp.int32)
    for a in range(tile_count):
        high = jnp.where(owner == a, places[a] // 16, high)
        low = jnp.where(owner == a, places[a] % 16, low)
        ocean = jnp.where(owner == a, rows[a], ocean)
    held[77:78, :] = high.astype(jnp.float32)
    held[78:79, :] = low.astype(jnp.float32)
    held[79:80, :] = ocean.astype(jnp.float32)
    out_ref[...] = held[...].astype(jnp.bfloat16)


def block_kernel(
    near, rows, gathered, x_ref, cot_ref, pick_ref, stem_ref, taps_ref, gain_ref, win_ref, wout_ref,
    out_ref, gin_ref, gout_ref, gker_ref, ggain_ref,
    sources, raw, padded, unit_s, inv_s, feats, hiddens, gpres, grads_t, gconv, kacc, gacc,
):
    f32 = jnp.float32
    bf16 = jnp.bfloat16
    tile_count, cin, _ = x_ref.shape
    chan = cot_ref.shape[1]
    lane_row = lax.broadcasted_iota(jnp.int32, (1, CELLS), 1) // TS
    kacc[...] = jnp.zeros_like(kacc)
    gacc[...] = jnp.zeros_like(gacc)
    sources[...] = jnp.zeros_like(sources)

    for a in range(tile_count):
        keep = (lane_row < rows[a]).astype(f32)
        tile = (x_ref[a].astype(f32) * keep).astype(bf16)
        sources[a, 0:cin, 0:CELLS] = tile
        for n in range(8):
            device = near[a, n, 0]
            slot = near[a, n, 1]
            block = gathered[device]
            piece = jnp.zeros((CINP, EDGE), bf16)
            for j in range(tile_count):
                piece = jnp.where(slot == j, block[:, j * EDGE : (j + 1) * EDGE], piece)
            sources[a, :, CELLS + n * EDGE : CELLS + (n + 1) * EDGE] = piece
    raw[...] = jnp.dot(
        sources[...].reshape(tile_count * CINP, KROWS), pick_ref[...], preferred_element_type=f32
    ).reshape(tile_count, CINP, PR * PC)

    @pl.loop(0, tile_count)
    def _(a):
        cells_in = raw[a].T.astype(bf16)
        stems = jnp.dot(cells_in, stem_ref[...], preferred_element_type=f32)
        padded[...] = stems.astype(bf16).astype(f32).reshape(PR, PC, chan)

        @pl.loop(0, TS // 4)
        def _(yb):
            y0 = yb * 4
            acc = jnp.zeros((4, TS, chan), f32)
            for k in range(KW):
                shifted = padded[pl.ds(y0, 4 + KW - 1), k : k + TS, :]
                for r in range(KW):
                    acc += taps_ref[r * KW + k : r * KW + k + 1, :][None] * shifted[r : r + 4]
            mean = jnp.mean(acc, axis=2, keepdims=True)
            centred = acc - mean
            inv = lax.rsqrt(jnp.mean(centred * centred, axis=2, keepdims=True) + 1e-06)
            unit_s[pl.ds(y0, 4)] = centred * inv
            inv_s[pl.ds(y0, 4)] = jnp.broadcast_to(inv, (4, TS, 128))

        gain = gain_ref[...]
        unit = unit_s[...].reshape(CELLS, chan)
        feat = (unit * gain).astype(bf16)
        feats[pl.ds(a * CELLS, CELLS), :] = feat
        pre = jnp.dot(feat, win_ref[...], preferred_element_type=f32)
        keep = (lane_row < rows[a]).astype(f32)
        mgrad_t = (cot_ref[a].astype(f32) * keep).astype(bf16)
        grads_t[a] = mgrad_t
        mgrad = mgrad_t.astype(f32).T.astype(bf16)
        ghid = lax.dot_general(mgrad, wout_ref[...], (((1,), (1,)), ((), ())), preferred_element_type=f32)
        square = pre * pre
        bend = jnp.tanh(0.7978845608028654 * pre * (1.0 + 0.044715 * square))
        half = 0.5 * (1.0 + bend)
        hidden = (pre * half).astype(bf16)
        slope = half + 0.5 * pre * (1.0 - bend * bend) * (0.7978845608028654 * (1.0 + 0.134145 * square))
        gpre = (ghid * slope).astype(bf16)
        hiddens[pl.ds(a * CELLS, CELLS), :] = hidden
        gpres[pl.ds(a * CELLS, CELLS), :] = gpre
        branch = jnp.dot(hidden, wout_ref[...], preferred_element_type=f32)
        stem_own = padded[REACH : REACH + TS, REACH : REACH + TS, :].reshape(CELLS, chan)
        out_ref[a] = ((stem_own + branch).T * keep).astype(bf16)
        gfeat = lax.dot_general(gpre, win_ref[...], (((1,), (1,)), ((), ())), preferred_element_type=f32)
        gfeat = gfeat.astype(bf16).astype(f32)
        gacc[...] += jnp.sum((gfeat * unit).reshape(CELLS // 8, 8, chan), axis=0)
        scaled = gfeat * gain
        first = jnp.mean(scaled, axis=1, keepdims=True)
        second = jnp.mean(scaled * unit, axis=1, keepdims=True)
        inv = inv_s[...].reshape(CELLS, 128)[:, 0:1]
        gconv[...] = (inv * (scaled - first - unit * second)).reshape(TS, TS, chan)

        @pl.loop(0, TS // 4)
        def _(yb):
            y0 = yb * 4
            grad = gconv[pl.ds(y0, 4)]
            for k in range(KW):
                shifted = padded[pl.ds(y0, 4 + KW - 1), k : k + TS, :]
                for r in range(KW):
                    prod = grad * shifted[r : r + 4]
                    kacc[r * KW + k] += jnp.sum(prod.reshape(8, 8, chan), axis=0)

    gin_ref[...] = lax.dot_general(
        feats[...], gpres[...], (((0,), (0,)), ((), ())), preferred_element_type=f32
    )
    total = jnp.zeros(gin_ref.shape, f32)
    for a in range(tile_count):
        total += jnp.dot(grads_t[a], hiddens[a * CELLS : (a + 1) * CELLS, :], preferred_element_type=f32)
    gout_ref[...] = total
    gker_ref[...] = jnp.sum(kacc[...], axis=1)
    ggain_ref[...] = jnp.sum(gacc[...], axis=0, keepdims=True)


def body(x_tiles, tile_pos, valid_rows, stem_w, dw_kernel, norm_gain, w_in, w_out, cotangent):
    f32 = jnp.float32
    bf16 = jnp.bfloat16
    lat_count = lax.axis_size("lat")
    lon_count = lax.axis_size("lon")
    inputs, places, rows, upstream = x_tiles[0], tile_pos[0], valid_rows[0], cotangent[0]
    tile_count, cin, _ = inputs.shape
    chan, hid = w_in.shape
    lanes = tile_count * EDGE
    smem = pl.BlockSpec(memory_space=pltpu.SMEM)
    vmem = pl.BlockSpec(memory_space=pltpu.VMEM)
    params = pltpu.CompilerParams(vmem_limit_bytes=VMEM_LIMIT)
    packed = pl.pallas_call(
        pack_kernel,
        out_shape=jax.ShapeDtypeStruct((CINP, lanes), bf16),
        in_specs=[smem, smem, vmem, vmem],
        out_specs=vmem,
        scratch_shapes=[pltpu.VMEM((CINP, lanes), f32)],
        compiler_params=params,
    )(places, rows, inputs, jnp.asarray(edge_pick(tile_count), bf16))
    gathered = lax.all_gather(packed, ("lon", "lat"))
    meta = gathered[:, 77:80, ::EDGE].astype(f32)
    all_place = (meta[:, 0, :] * 16.0 + meta[:, 1, :]).astype(jnp.int32)
    cell_total = TS * jnp.sum(meta[:, 2, :])
    count = lon_count * lat_count
    sector = jnp.arange(count, dtype=jnp.int32)[:, None] // lat_count
    row_all = all_place // TCOLS
    col_all = sector * TCOLS + all_place % TCOLS
    key_all = (row_all * (TCOLS * lon_count) + col_all).reshape(-1)
    off = np.array(OFFSETS, np.int32)
    my_row = places // TCOLS
    my_col = lax.axis_index("lon") * TCOLS + places % TCOLS
    want_row = my_row[:, None] + off[None, :, 0]
    want_col = (my_col[:, None] + off[None, :, 1]) % (TCOLS * lon_count)
    want = want_row * (TCOLS * lon_count) + want_col
    hit = want[:, :, None] == key_all[None, None, :]
    where = jnp.sum(jnp.where(hit, jnp.arange(count * tile_count, dtype=jnp.int32) + 1, 0), axis=2) - 1
    near = jnp.stack(
        [jnp.maximum(where, 0) // tile_count, jnp.where(where < 0, -1, where % tile_count)], axis=2
    )
    outs = pl.pallas_call(
        block_kernel,
        out_shape=[
            jax.ShapeDtypeStruct((tile_count, chan, CELLS), bf16),
            jax.ShapeDtypeStruct((chan, hid), f32),
            jax.ShapeDtypeStruct((chan, hid), f32),
            jax.ShapeDtypeStruct((KW * KW, chan), f32),
            jax.ShapeDtypeStruct((1, chan), f32),
        ],
        in_specs=[smem, smem] + [vmem] * 9,
        out_specs=[vmem] * 5,
        scratch_shapes=[
            pltpu.VMEM((tile_count, CINP, KROWS), bf16),
            pltpu.VMEM((tile_count, CINP, PR * PC), f32),
            pltpu.VMEM((PR, PC, chan), f32),
            pltpu.VMEM((TS, TS, chan), f32),
            pltpu.VMEM((TS, TS, 128), f32),
            pltpu.VMEM((tile_count * CELLS, chan), bf16),
            pltpu.VMEM((tile_count * CELLS, hid), bf16),
            pltpu.VMEM((tile_count * CELLS, hid), bf16),
            pltpu.VMEM((tile_count, chan, CELLS), bf16),
            pltpu.VMEM((TS, TS, chan), f32),
            pltpu.VMEM((KW * KW, 8, chan), f32),
            pltpu.VMEM((8, chan), f32),
        ],
        compiler_params=params,
    )(
        near, rows, gathered, inputs, upstream, jnp.asarray(halo_pick(), bf16),
        jnp.pad(stem_w, ((0, CINP - cin), (0, 0))), dw_kernel.T, norm_gain[None], w_in, w_out,
    )
    result, sum_in, sum_out, sum_kernel, sum_gain = outs
    sums = lax.psum((sum_in, sum_out, sum_kernel, sum_gain), ("lat", "lon"))
    scale = 1.0 / cell_total
    return (
        result[None],
        sums[0] * scale,
        sums[1].T * scale,
        sums[2].T * scale,
        sums[3][0] * scale,
    )


def solution(mesh):
    in_specs = (
        P("lon", "lat", None, None),
        P("lon", "lat"),
        P("lon", "lat"),
        P(),
        P(),
        P(),
        P(),
        P(),
        P("lon", "lat", None, None),
    )
    out_specs = (P("lon", "lat", None, None), P(), P(), P(), P())
    return jax.shard_map(body, mesh=mesh, in_specs=in_specs, out_specs=out_specs, check_vma=False)
```

```python
import functools

import jax
import jax.numpy as jnp
import numpy as np
from jax import lax
from jax.experimental import pallas as pl
from jax.experimental.pallas import tpu as pltpu
from jax.sharding import PartitionSpec as P

TS = 16
CELLS = TS * TS
KW = 7
REACH = KW // 2
TCOLS = 8
EDGE = 160
PR = TS + 2 * REACH
PC = 24
CINP = 80
KROWS = CELLS + 8 * EDGE
OFFSETS = ((-1, -1), (-1, 0), (-1, 1), (0, -1), (0, 1), (1, -1), (1, 0), (1, 1))
SIDE = 896
WIDE = 2 * SIDE
ROWT = 13
USED = ROWT * WIDE // 128
VMEM_LIMIT = 56 * 1024 * 1024


def edge_index():
    table = -np.ones((TS, TS), np.int64)
    count = 0
    for y in range(TS):
        for x in range(TS):
            if min(y, x) < REACH or max(y, x) >= TS - REACH:
                table[y, x] = count
                count += 1
    return table


def edge_pick(tile_count):
    table = edge_index()
    pick = np.zeros((tile_count, CELLS, tile_count * EDGE), np.float32)
    for y in range(TS):
        for x in range(TS):
            if table[y, x] >= 0:
                for a in range(tile_count):
                    pick[a, y * TS + x, a * EDGE + table[y, x]] = 1
    return pick


def halo_pick():
    table = edge_index()
    pick = np.zeros((KROWS, PR * PC), np.float32)
    for py in range(PR):
        for px in range(PR):
            y, x = py - REACH, px - REACH
            dy, dx = y // TS, x // TS
            cell = py * PC + px
            if (dy, dx) == (0, 0):
                pick[y * TS + x, cell] = 1
            else:
                n = OFFSETS.index((dy, dx))
                pick[CELLS + n * EDGE + table[y % TS, x % TS], cell] = 1
    return pick


def pack_kernel(places, rows, x_ref, pick_ref, out_ref, held):
    tile_count = x_ref.shape[0]
    lanes = tile_count * EDGE
    cell_row = lax.broadcasted_iota(jnp.int32, (1, CELLS), 1) // TS
    total = jnp.zeros((x_ref.shape[1], lanes), jnp.float32)
    for a in range(tile_count):
        keep = (cell_row < rows[a]).astype(jnp.float32)
        tile = (x_ref[a].astype(jnp.float32) * keep).astype(jnp.bfloat16)
        total += jnp.dot(tile, pick_ref[a], preferred_element_type=jnp.float32)
    held[...] = jnp.zeros_like(held)
    held[0 : x_ref.shape[1], :] = total
    owner = lax.broadcasted_iota(jnp.int32, (1, lanes), 1) // EDGE
    high = jnp.zeros((1, lanes), jnp.int32)
    low = jnp.zeros((1, lanes), jnp.int32)
    ocean = jnp.zeros((1, lanes), jnp.int32)
    for a in range(tile_count):
        high = jnp.where(owner == a, places[a] // 16, high)
        low = jnp.where(owner == a, places[a] % 16, low)
        ocean = jnp.where(owner == a, rows[a], ocean)
    held[77:78, :] = high.astype(jnp.float32)
    held[78:79, :] = low.astype(jnp.float32)
    held[79:80, :] = ocean.astype(jnp.float32)
    out_ref[...] = held[...].astype(jnp.bfloat16)


def block_kernel(
    near, rows, gathered, x_ref, cot_ref, pick_ref, stem_ref, taps_ref, gain_ref, win_ref, wout_ref,
    out_ref, pack_ref,
    held, small, sources, raw, padded, unit_s, inv_s, feats, hiddens, gpres, grads_t, gconv, kacc, gacc,
):
    f32 = jnp.float32
    bf16 = jnp.bfloat16
    tile_count, cin, _ = x_ref.shape
    chan = cot_ref.shape[1]
    lane_row = lax.broadcasted_iota(jnp.int32, (1, CELLS), 1) // TS
    kacc[...] = jnp.zeros_like(kacc)
    gacc[...] = jnp.zeros_like(gacc)
    sources[...] = jnp.zeros_like(sources)

    for a in range(tile_count):
        keep = (lane_row < rows[a]).astype(f32)
        tile = (x_ref[a].astype(f32) * keep).astype(bf16)
        sources[a, 0:cin, 0:CELLS] = tile
        for n in range(8):
            device = near[a, n, 0]
            slot = near[a, n, 1]
            block = gathered[device]
            piece = jnp.zeros((CINP, EDGE), bf16)
            for j in range(tile_count):
                piece = jnp.where(slot == j, block[:, j * EDGE : (j + 1) * EDGE], piece)
            sources[a, :, CELLS + n * EDGE : CELLS + (n + 1) * EDGE] = piece
    raw[...] = jnp.dot(
        sources[...].reshape(tile_count * CINP, KROWS), pick_ref[...], preferred_element_type=f32
    ).reshape(tile_count, CINP, PR * PC)

    @pl.loop(0, tile_count)
    def _(a):
        cells_in = raw[a].T.astype(bf16)
        stems = jnp.dot(cells_in, stem_ref[...], preferred_element_type=f32)
        padded[...] = stems.astype(bf16).astype(f32).reshape(PR, PC, chan)

        @pl.loop(0, TS // 4)
        def _(yb):
            y0 = yb * 4
            acc = jnp.zeros((4, TS, chan), f32)
            for k in range(KW):
                shifted = padded[pl.ds(y0, 4 + KW - 1), k : k + TS, :]
                for r in range(KW):
                    acc += taps_ref[r * KW + k : r * KW + k + 1, :][None] * shifted[r : r + 4]
            mean = jnp.mean(acc, axis=2, keepdims=True)
            centred = acc - mean
            inv = lax.rsqrt(jnp.mean(centred * centred, axis=2, keepdims=True) + 1e-06)
            unit_s[pl.ds(y0, 4)] = centred * inv
            inv_s[pl.ds(y0, 4)] = jnp.broadcast_to(inv, (4, TS, 128))

        gain = gain_ref[...]
        unit = unit_s[...].reshape(CELLS, chan)
        feat = (unit * gain).astype(bf16)
        feats[pl.ds(a * CELLS, CELLS), :] = feat
        pre = jnp.dot(feat, win_ref[...], preferred_element_type=f32)
        keep = (lane_row < rows[a]).astype(f32)
        mgrad_t = (cot_ref[a].astype(f32) * keep).astype(bf16)
        grads_t[a] = mgrad_t
        mgrad = mgrad_t.astype(f32).T.astype(bf16)
        ghid = lax.dot_general(mgrad, wout_ref[...], (((1,), (1,)), ((), ())), preferred_element_type=f32)
        square = pre * pre
        bend = jnp.tanh(0.7978845608028654 * pre * (1.0 + 0.044715 * square))
        half = 0.5 * (1.0 + bend)
        hidden = (pre * half).astype(bf16)
        slope = half + 0.5 * pre * (1.0 - bend * bend) * (0.7978845608028654 * (1.0 + 0.134145 * square))
        gpre = (ghid * slope).astype(bf16)
        hiddens[pl.ds(a * CELLS, CELLS), :] = hidden
        gpres[pl.ds(a * CELLS, CELLS), :] = gpre
        branch = jnp.dot(hidden, wout_ref[...], preferred_element_type=f32)
        stem_own = padded[REACH : REACH + TS, REACH : REACH + TS, :].reshape(CELLS, chan)
        out_ref[a] = ((stem_own + branch).T * keep).astype(bf16)
        gfeat = lax.dot_general(gpre, win_ref[...], (((1,), (1,)), ((), ())), preferred_element_type=f32)
        gfeat = gfeat.astype(bf16).astype(f32)
        gacc[...] += jnp.sum((gfeat * unit).reshape(CELLS // 8, 8, chan), axis=0)
        scaled = gfeat * gain
        first = jnp.mean(scaled, axis=1, keepdims=True)
        second = jnp.mean(scaled * unit, axis=1, keepdims=True)
        inv = inv_s[...].reshape(CELLS, 128)[:, 0:1]
        gconv[...] = (inv * (scaled - first - unit * second)).reshape(TS, TS, chan)

        @pl.loop(0, TS // 4)
        def _(yb):
            y0 = yb * 4
            grad = gconv[pl.ds(y0, 4)]
            for k in range(KW):
                shifted = padded[pl.ds(y0, 4 + KW - 1), k : k + TS, :]
                for r in range(KW):
                    prod = grad * shifted[r : r + 4]
                    kacc[r * KW + k] += jnp.sum(prod.reshape(8, 8, chan), axis=0)

    held[...] = jnp.zeros_like(held)
    small[...] = jnp.zeros_like(small)
    hid = win_ref.shape[1]
    held[0:chan, 0:hid] = lax.dot_general(
        feats[...], gpres[...], (((0,), (0,)), ((), ())), preferred_element_type=f32
    )
    total = jnp.zeros((chan, hid), f32)
    for a in range(tile_count):
        total += jnp.dot(grads_t[a], hiddens[a * CELLS : (a + 1) * CELLS, :], preferred_element_type=f32)
    held[0:chan, SIDE : SIDE + hid] = total
    small[0 : KW * KW, 0:chan] = jnp.sum(kacc[...], axis=1)
    small[KW * KW : KW * KW + 1, 0:chan] = jnp.sum(gacc[...], axis=0, keepdims=True)
    held[0:chan, hid:SIDE] = small[...].T[0:chan, 0 : SIDE - hid]
    for t in range(WIDE // 128):
        part = held[:, t * 128 : (t + 1) * 128].astype(bf16)
        pack_ref[t * ROWT : (t + 1) * ROWT] = part.reshape(ROWT, 16, 128)
    spare = pack_ref.shape[0] - USED
    pack_ref[USED:] = jnp.zeros((spare, 16, 128), bf16)


def unpack_kernel(total_ref, tiles_ref, gin_ref, gout_ref, gker_ref, ggain_ref, held):
    scale = 1.0 / total_ref[0]
    chan, hid = gin_ref.shape
    for t in range(WIDE // 128):
        part = tiles_ref[t * ROWT : (t + 1) * ROWT].astype(jnp.float32) * scale
        held[:, t * 128 : (t + 1) * 128] = part.reshape(ROWT * 16, 128)
    gin_ref[...] = held[0:chan, 0:hid]
    gout_ref[...] = held[:, SIDE:WIDE].T[0:hid, 0:chan]
    gker_ref[...] = held[0:chan, hid : hid + KW * KW]
    base = SIDE - 128
    flipped = held[:, base:SIDE].T
    row = hid + KW * KW - base
    ggain_ref[...] = flipped[row : row + 1, 0:chan]


def greet(devices):
    barrier = pltpu.get_barrier_semaphore()
    for device in devices:
        pl.semaphore_signal(barrier, inc=1, device_id=device, device_id_type=pl.DeviceIdType.MESH)
    pl.semaphore_wait(barrier, len(devices))


def gather_kernel(with_lon, src, out, send_sem, recv_sem, own_sem):
    lat, lon = lax.axis_index("lat"), lax.axis_index("lon")
    z, x, core = lat // 4, (lat // 2) % 2, lat % 2

    def coords(step):
        dz, dx, dy, dc = step
        where = ((z + dz) % 4) * 4 + ((x + dx) % 2) * 2 + (core + dc) % 2
        return where, (lon + dy) % 2 if with_lon else lon

    def place(step):
        where, sector = coords(step)
        return sector * 16 + where if with_lon else where

    def device_of(step):
        where, sector = coords(step)
        return {"lat": where, "lon": sector}

    def number(step):
        dz, dx, dy, dc = step
        return ((dz * 2 + dx) * 2 + dy) * 2 + dc

    peers = [(1, 0, 0, 0), (2, 0, 0, 0), (3, 0, 0, 0), (0, 1, 0, 0), (0, 0, 0, 1)]
    if with_lon:
        peers.append((0, 0, 1, 0))
    greet([device_of(p) for p in peers])
    copies = {}

    def send(block, hop, landed):
        here = src if block == (0, 0, 0, 0) else out.at[place(block)]
        n = number(landed)
        copy = pltpu.make_async_remote_copy(
            src_ref=here, dst_ref=out.at[place(block)], send_sem=send_sem.at[n],
            recv_sem=recv_sem.at[n], device_id=device_of(hop), device_id_type=pl.DeviceIdType.MESH,
        )
        copy.start()
        copies[landed] = copy

    def forward(block):
        dz, dx, dy, dc = block
        if dx == 0 and dy == 0:
            send(block, (0, 1, 0, 0), (dz, 1, 0, 0))
        if with_lon and dy == 0:
            send(block, (0, 0, 1, 0), (dz, dx, 1, 0))
        send(block, (0, 0, 0, 1), (dz, dx, dy, 1))

    own = pltpu.make_async_copy(src, out.at[place((0, 0, 0, 0))], own_sem)
    for dz in (1, 3, 2):
        send((0, 0, 0, 0), (dz, 0, 0, 0), ((4 - dz) % 4, 0, 0, 0))
    forward((0, 0, 0, 0))
    own.start()
    order = [(0, 1), (1, 0), (3, 0), (1, 1), (3, 1), (2, 0), (2, 1)]
    blocks = [(dz, dx, 0, 0) for dz, dx in order]
    if with_lon:
        blocks += [(dz, dx, 1, 0) for dz, dx in [(0, 0)] + order]
    for block in blocks:
        copies[block].wait_recv()
        forward(block)
    for landed, copy in copies.items():
        if landed[3] == 1:
            copy.wait_recv()
    for copy in copies.values():
        copy.wait_send()
    own.wait()


def reduce_kernel(n_lon, per, src, out, first, acc, second, third, sems):
    lat, lon = lax.axis_index("lat"), lax.axis_index("lon")
    z = lat // 4
    groups, deep = n_lon * 4, 4
    span = per * deep
    mine = lon * 4 + lat % 4

    def in_plane(d):
        g = (mine + d) % groups
        return g, {"lat": z * 4 + g % 4, "lon": g // 4}

    def along(d):
        other = (z + d) % deep
        return other, {"lat": other * 4 + lat % 4, "lon": lon}

    greet([in_plane(d)[1] for d in range(1, groups)] + [along(d)[1] for d in range(1, deep)])
    copies = []

    def send(stage, back, here, there, device):
        copy = pltpu.make_async_remote_copy(
            src_ref=here, dst_ref=there, send_sem=sems.at[stage, 0, back], recv_sem=sems.at[stage, 1, back],
            device_id=device, device_id_type=pl.DeviceIdType.MESH,
        )
        copy.start()
        copies.append(copy)
        return copy

    landing = []
    for d in range(1, groups):
        g, device = in_plane(d)
        landing.append(send(0, groups - d, src.at[pl.ds(g * span, span)], first.at[groups - d], device))
    acc[...] = src[pl.ds(mine * span, span)].astype(jnp.float32)
    for d in range(1, groups):
        landing[d - 1].wait_recv()
        acc[...] += first[groups - d].astype(jnp.float32)
    second[...] = acc[...].astype(jnp.bfloat16)
    landing = []
    for d in range(1, deep):
        other, device = along(d)
        landing.append(send(1, deep - d, second.at[pl.ds(other * per, per)], third.at[deep - d], device))
    total = acc[pl.ds(z * per, per)]
    for d in range(1, deep):
        landing[d - 1].wait_recv()
        total += third[deep - d].astype(jnp.float32)
    mark = pl.ds(mine * span + z * per, per)
    out[mark] = total.astype(jnp.bfloat16)
    landing = []
    for d in range(1, deep):
        landing.append(send(2, deep - d, out.at[mark], out.at[mark], along(d)[1]))
    for copy in landing:
        copy.wait_recv()
    whole = pl.ds(mine * span, span)
    landing = []
    for d in range(1, groups):
        landing.append(send(3, groups - d, out.at[whole], out.at[whole], in_plane(d)[1]))
    for copy in landing:
        copy.wait_recv()
    for copy in copies:
        copy.wait_send()


def body(x_tiles, tile_pos, valid_rows, stem_w, dw_kernel, norm_gain, w_in, w_out, cotangent):
    f32 = jnp.float32
    bf16 = jnp.bfloat16
    lat_count = lax.axis_size("lat")
    lon_count = lax.axis_size("lon")
    inputs, places, rows, upstream = x_tiles[0], tile_pos[0], valid_rows[0], cotangent[0]
    tile_count, cin, _ = inputs.shape
    chan, hid = w_in.shape
    lanes = tile_count * EDGE
    smem = pl.BlockSpec(memory_space=pltpu.SMEM)
    vmem = pl.BlockSpec(memory_space=pltpu.VMEM)
    params = pltpu.CompilerParams(vmem_limit_bytes=VMEM_LIMIT)
    packed = pl.pallas_call(
        pack_kernel,
        out_shape=jax.ShapeDtypeStruct((CINP, lanes), bf16),
        in_specs=[smem, smem, vmem, vmem],
        out_specs=vmem,
        scratch_shapes=[pltpu.VMEM((CINP, lanes), f32)],
        compiler_params=params,
    )(places, rows, inputs, jnp.asarray(edge_pick(tile_count), bf16))
    with_lon = lon_count == 2
    blocks = 32 if with_lon else 16
    gathered = pl.pallas_call(
        functools.partial(gather_kernel, with_lon),
        out_shape=jax.ShapeDtypeStruct((blocks, CINP, lanes), bf16),
        in_specs=[vmem],
        out_specs=vmem,
        scratch_shapes=[
            pltpu.SemaphoreType.DMA((32,)),
            pltpu.SemaphoreType.DMA((32,)),
            pltpu.SemaphoreType.DMA,
        ],
        compiler_params=pltpu.CompilerParams(
            vmem_limit_bytes=VMEM_LIMIT, collective_id=0, has_side_effects=True
        ),
    )(packed)
    if not with_lon:
        gathered = lax.all_gather(gathered, "lon", tiled=True)
    meta = gathered[:, 77:80, ::EDGE].astype(f32)
    all_place = (meta[:, 0, :] * 16.0 + meta[:, 1, :]).astype(jnp.int32)
    cell_total = TS * jnp.sum(meta[:, 2, :])
    count = lon_count * lat_count
    sector = jnp.arange(count, dtype=jnp.int32)[:, None] // lat_count
    row_all = all_place // TCOLS
    col_all = sector * TCOLS + all_place % TCOLS
    key_all = (row_all * (TCOLS * lon_count) + col_all).reshape(-1)
    off = np.array(OFFSETS, np.int32)
    my_row = places // TCOLS
    my_col = lax.axis_index("lon") * TCOLS + places % TCOLS
    want_row = my_row[:, None] + off[None, :, 0]
    want_col = (my_col[:, None] + off[None, :, 1]) % (TCOLS * lon_count)
    want = want_row * (TCOLS * lon_count) + want_col
    hit = want[:, :, None] == key_all[None, None, :]
    where = jnp.sum(jnp.where(hit, jnp.arange(count * tile_count, dtype=jnp.int32) + 1, 0), axis=2) - 1
    near = jnp.stack(
        [jnp.maximum(where, 0) // tile_count, jnp.where(where < 0, -1, where % tile_count)], axis=2
    )
    groups = lon_count * 4
    per = -(-USED // (groups * 4))
    tiles_all = per * groups * 4
    result, packed_sums = pl.pallas_call(
        block_kernel,
        out_shape=[
            jax.ShapeDtypeStruct((tile_count, chan, CELLS), bf16),
            jax.ShapeDtypeStruct((tiles_all, 16, 128), bf16),
        ],
        in_specs=[smem, smem] + [vmem] * 9,
        out_specs=[vmem] * 2,
        scratch_shapes=[
            pltpu.VMEM((ROWT * 16, WIDE), f32),
            pltpu.VMEM((128, 256), f32),
            pltpu.VMEM((tile_count, CINP, KROWS), bf16),
            pltpu.VMEM((tile_count, CINP, PR * PC), f32),
            pltpu.VMEM((PR, PC, chan), f32),
            pltpu.VMEM((TS, TS, chan), f32),
            pltpu.VMEM((TS, TS, 128), f32),
            pltpu.VMEM((tile_count * CELLS, chan), bf16),
            pltpu.VMEM((tile_count * CELLS, hid), bf16),
            pltpu.VMEM((tile_count * CELLS, hid), bf16),
            pltpu.VMEM((tile_count, chan, CELLS), bf16),
            pltpu.VMEM((TS, TS, chan), f32),
            pltpu.VMEM((KW * KW, 8, chan), f32),
            pltpu.VMEM((8, chan), f32),
        ],
        compiler_params=params,
    )(
        near, rows, gathered, inputs, upstream, jnp.asarray(halo_pick(), bf16),
        jnp.pad(stem_w, ((0, CINP - cin), (0, 0))), dw_kernel.T, norm_gain[None], w_in, w_out,
    )
    span = per * 4
    reduced = pl.pallas_call(
        functools.partial(reduce_kernel, lon_count, per),
        out_shape=jax.ShapeDtypeStruct((tiles_all, 16, 128), bf16),
        in_specs=[vmem],
        out_specs=vmem,
        scratch_shapes=[
            pltpu.VMEM((groups, span, 16, 128), bf16),
            pltpu.VMEM((span, 16, 128), f32),
            pltpu.VMEM((span, 16, 128), bf16),
            pltpu.VMEM((4, per, 16, 128), bf16),
            pltpu.SemaphoreType.DMA((4, 2, groups)),
        ],
        compiler_params=pltpu.CompilerParams(
            vmem_limit_bytes=VMEM_LIMIT, collective_id=1, has_side_effects=True
        ),
    )(packed_sums)
    sum_in, sum_out, sum_kernel, sum_gain = pl.pallas_call(
        unpack_kernel,
        out_shape=[
            jax.ShapeDtypeStruct((chan, hid), f32),
            jax.ShapeDtypeStruct((hid, chan), f32),
            jax.ShapeDtypeStruct((chan, KW * KW), f32),
            jax.ShapeDtypeStruct((1, chan), f32),
        ],
        in_specs=[smem, vmem],
        out_specs=[vmem] * 4,
        scratch_shapes=[pltpu.VMEM((ROWT * 16, WIDE), f32)],
        compiler_params=params,
    )(cell_total.reshape(1), reduced)
    return result[None], sum_in, sum_out, sum_kernel, sum_gain[0]


def solution(mesh):
    in_specs = (
        P("lon", "lat", None, None),
        P("lon", "lat"),
        P("lon", "lat"),
        P(),
        P(),
        P(),
        P(),
        P(),
        P("lon", "lat", None, None),
    )
    out_specs = (P("lon", "lat", None, None), P(), P(), P(), P())
    return jax.shard_map(body, mesh=mesh, in_specs=in_specs, out_specs=out_specs, check_vma=False)
```

```python
import functools

import jax
import jax.numpy as jnp
import numpy as np
from jax import lax
from jax.experimental import pallas as pl
from jax.experimental.pallas import tpu as pltpu
from jax.sharding import PartitionSpec as P

TS = 16
CELLS = TS * TS
KW = 7
REACH = KW // 2
TCOLS = 8
EDGE = 160
PR = TS + 2 * REACH
PC = 24
CINP = 80
SIDE_CELLS = 64
KEDGE = CELLS + 8 * EDGE
OFFSETS = ((-1, -1), (-1, 0), (-1, 1), (0, -1), (0, 1), (1, -1), (1, 0), (1, 1))
SIDE = 896
WIDE = 2 * SIDE
ROWT = 13
USED = ROWT * WIDE // 128
CROSS = tuple(n for n, (dy, dx) in enumerate(OFFSETS) if dx != 0)
VMEM_LIMIT = 56 * 1024 * 1024


def edge_index():
    table = -np.ones((TS, TS), np.int64)
    count = 0
    for y in range(TS):
        for x in range(TS):
            if min(y, x) < REACH or max(y, x) >= TS - REACH:
                table[y, x] = count
                count += 1
    return table


def edge_pick():
    table = edge_index()
    pick = np.zeros((CELLS, EDGE), np.float32)
    for y in range(TS):
        for x in range(TS):
            if table[y, x] >= 0:
                pick[y * TS + x, table[y, x]] = 1
    return pick


def side_pick():
    pick = np.zeros((2, CELLS, SIDE_CELLS), np.float32)
    for y in range(TS):
        for x in range(REACH):
            pick[0, y * TS + x, y * REACH + x] = 1
            pick[1, y * TS + TS - REACH + x, y * REACH + x] = 1
    return pick


def halo_pick(with_lon):
    table = edge_index()
    pick = np.zeros((KEDGE + 6 * SIDE_CELLS * with_lon, PR * PC), np.float32)
    for py in range(PR):
        for px in range(PR):
            y, x = py - REACH, px - REACH
            dy, dx = y // TS, x // TS
            cell = py * PC + px
            if (dy, dx) == (0, 0):
                pick[y * TS + x, cell] = 1
            else:
                n = OFFSETS.index((dy, dx))
                pick[CELLS + n * EDGE + table[y % TS, x % TS], cell] = 1
                if with_lon and dx != 0:
                    part = (y % TS) * REACH + (x % TS if dx > 0 else x % TS - TS + REACH)
                    pick[KEDGE + CROSS.index(n) * SIDE_CELLS + part, cell] = 1
    return pick


def pack_kernel(places, rows, x_ref, pick_ref, side_ref, out_ref, out_side_ref, held, held_side):
    tile_count, cin, _ = x_ref.shape
    cell_row = lax.broadcasted_iota(jnp.int32, (1, CELLS), 1) // TS
    held[...] = jnp.zeros_like(held)
    held_side[...] = jnp.zeros_like(held_side)
    for a in range(tile_count):
        keep = (cell_row < rows[a]).astype(jnp.float32)
        tile = (x_ref[a].astype(jnp.float32) * keep).astype(jnp.bfloat16)
        held[0:cin, a * EDGE : (a + 1) * EDGE] = jnp.dot(
            tile, pick_ref[...], preferred_element_type=jnp.float32
        )
        outer = jnp.where((places[a] & (TCOLS - 1)) == 0, side_ref[0], side_ref[1])
        held_side[0:cin, a * SIDE_CELLS : (a + 1) * SIDE_CELLS] = jnp.dot(
            tile, outer, preferred_element_type=jnp.float32
        )
    owner = lax.broadcasted_iota(jnp.int32, (1, 128), 1)
    high = jnp.zeros((1, 128), jnp.int32)
    low = jnp.zeros((1, 128), jnp.int32)
    ocean = jnp.zeros((1, 128), jnp.int32)
    for a in range(tile_count):
        high = jnp.where(owner == a, places[a] >> 4, high)
        low = jnp.where(owner == a, places[a] & 15, low)
        ocean = jnp.where(owner == a, rows[a], ocean)
    for target in (held, held_side):
        target[77:78, 0:128] = high.astype(jnp.float32)
        target[78:79, 0:128] = low.astype(jnp.float32)
        target[79:80, 0:128] = ocean.astype(jnp.float32)
    out_ref[...] = held[...].astype(jnp.bfloat16)
    out_side_ref[...] = held_side[...].astype(jnp.bfloat16)


def block_kernel(
    with_lon, near, rows, gathered, sides, x_ref, cot_ref, pick_ref, stem_ref, taps_ref, gain_ref, win_ref, wout_ref,
    out_ref, pack_ref,
    held, small, stem_s, sources, raw, padded, unit_s, inv_s, feats, hiddens, gpres, grads_t, gconv, kacc, gacc,
):
    f32 = jnp.float32
    bf16 = jnp.bfloat16
    tile_count, cin, _ = x_ref.shape
    chan = cot_ref.shape[1]
    lane_row = lax.broadcasted_iota(jnp.int32, (1, CELLS), 1) // TS
    kacc[...] = jnp.zeros_like(kacc)
    gacc[...] = jnp.zeros_like(gacc)
    sources[...] = jnp.zeros_like(sources)
    stem_s[...] = jnp.zeros_like(stem_s)
    stem_s[0:cin, :] = stem_ref[...]

    for a in range(tile_count):
        keep = (lane_row < rows[a]).astype(f32)
        tile = (x_ref[a].astype(f32) * keep).astype(bf16)
        sources[a, 0:cin, 0:CELLS] = tile
        for n in range(8):
            code = near[a, n]
            slot = code & 7
            block = gathered[code >> 3]
            piece = jnp.zeros((CINP, EDGE), bf16)
            for j in range(tile_count):
                piece = jnp.where(slot == j, block[:, j * EDGE : (j + 1) * EDGE], piece)
            sources[a, :, CELLS + n * EDGE : CELLS + (n + 1) * EDGE] = piece
        for m, n in enumerate(CROSS if with_lon else ()):
            code = near[a, 8 + n]
            slot = code & 7
            block = sides[code >> 3]
            piece = jnp.zeros((CINP, SIDE_CELLS), bf16)
            for j in range(tile_count):
                piece = jnp.where(slot == j, block[:, j * SIDE_CELLS : (j + 1) * SIDE_CELLS], piece)
            start = KEDGE + m * SIDE_CELLS
            sources[a, :, start : start + SIDE_CELLS] = piece
    raw[...] = jnp.dot(
        sources[...].reshape(tile_count * CINP, pick_ref.shape[0]), pick_ref[...], preferred_element_type=f32
    ).reshape(tile_count, CINP, PR * PC)

    @pl.loop(0, tile_count)
    def _(a):
        cells_in = raw[a].T.astype(bf16)
        stems = jnp.dot(cells_in, stem_s[...], preferred_element_type=f32)
        padded[...] = stems.astype(bf16).astype(f32).reshape(PR, PC, chan)

        @pl.loop(0, TS // 4)
        def _(yb):
            y0 = yb * 4
            acc = jnp.zeros((4, TS, chan), f32)
            for k in range(KW):
                shifted = padded[pl.ds(y0, 4 + KW - 1), k : k + TS, :]
                for r in range(KW):
                    acc += taps_ref[r * KW + k : r * KW + k + 1, :][None] * shifted[r : r + 4]
            mean = jnp.mean(acc, axis=2, keepdims=True)
            centred = acc - mean
            inv = lax.rsqrt(jnp.mean(centred * centred, axis=2, keepdims=True) + 1e-06)
            unit_s[pl.ds(y0, 4)] = centred * inv
            inv_s[pl.ds(y0, 4)] = jnp.broadcast_to(inv, (4, TS, 128))

        gain = gain_ref[...]
        unit = unit_s[...].reshape(CELLS, chan)
        feat = (unit * gain).astype(bf16)
        feats[pl.ds(a * CELLS, CELLS), :] = feat
        pre = jnp.dot(feat, win_ref[...], preferred_element_type=f32)
        keep = (lane_row < rows[a]).astype(f32)
        mgrad_t = (cot_ref[a].astype(f32) * keep).astype(bf16)
        grads_t[a] = mgrad_t
        mgrad = mgrad_t.astype(f32).T.astype(bf16)
        ghid = jnp.dot(mgrad, wout_ref[...], preferred_element_type=f32)
        square = pre * pre
        bend = jnp.tanh(0.7978845608028654 * pre * (1.0 + 0.044715 * square))
        half = 0.5 * (1.0 + bend)
        hidden = (pre * half).astype(bf16)
        slope = half + 0.5 * pre * (1.0 - bend * bend) * (0.7978845608028654 * (1.0 + 0.134145 * square))
        gpre = (ghid * slope).astype(bf16)
        hiddens[pl.ds(a * CELLS, CELLS), :] = hidden
        gpres[pl.ds(a * CELLS, CELLS), :] = gpre
        branch = lax.dot_general(
            hidden, wout_ref[...], (((1,), (1,)), ((), ())), preferred_element_type=f32
        )
        stem_own = padded[REACH : REACH + TS, REACH : REACH + TS, :].reshape(CELLS, chan)
        out_ref[a] = ((stem_own + branch).T * keep).astype(bf16)
        gfeat = lax.dot_general(gpre, win_ref[...], (((1,), (1,)), ((), ())), preferred_element_type=f32)
        gfeat = gfeat.astype(bf16).astype(f32)
        gacc[...] += jnp.sum((gfeat * unit).reshape(CELLS // 8, 8, chan), axis=0)
        scaled = gfeat * gain
        first = jnp.mean(scaled, axis=1, keepdims=True)
        second = jnp.mean(scaled * unit, axis=1, keepdims=True)
        inv = inv_s[...].reshape(CELLS, 128)[:, 0:1]
        gconv[...] = (inv * (scaled - first - unit * second)).reshape(TS, TS, chan)

        @pl.loop(0, TS // 4)
        def _(yb):
            y0 = yb * 4
            grad = gconv[pl.ds(y0, 4)]
            for k in range(KW):
                shifted = padded[pl.ds(y0, 4 + KW - 1), k : k + TS, :]
                for r in range(KW):
                    prod = grad * shifted[r : r + 4]
                    kacc[r * KW + k] += jnp.sum(prod.reshape(8, 8, chan), axis=0)

    held[...] = jnp.zeros_like(held)
    small[...] = jnp.zeros_like(small)
    hid = win_ref.shape[1]
    held[0:chan, 0:hid] = lax.dot_general(
        feats[...], gpres[...], (((0,), (0,)), ((), ())), preferred_element_type=f32
    )
    total = jnp.zeros((chan, hid), f32)
    for a in range(tile_count):
        total += jnp.dot(grads_t[a], hiddens[a * CELLS : (a + 1) * CELLS, :], preferred_element_type=f32)
    held[0:chan, SIDE : SIDE + hid] = total
    small[0 : KW * KW, 0:chan] = jnp.sum(kacc[...], axis=1)
    small[KW * KW : KW * KW + 1, 0:chan] = jnp.sum(gacc[...], axis=0, keepdims=True)
    held[0:chan, hid:SIDE] = small[...].T[0:chan, 0 : SIDE - hid]
    for t in range(WIDE // 128):
        part = held[:, t * 128 : (t + 1) * 128].astype(bf16)
        pack_ref[t * ROWT : (t + 1) * ROWT] = part.reshape(ROWT, 16, 128)
    spare = pack_ref.shape[0] - USED
    pack_ref[USED:] = jnp.zeros((spare, 16, 128), bf16)


def unpack_kernel(total_ref, tiles_ref, gin_ref, gout_ref, gker_ref, ggain_ref, held):
    scale = 1.0 / total_ref[0]
    chan, hid = gin_ref.shape
    for t in range(WIDE // 128):
        part = tiles_ref[t * ROWT : (t + 1) * ROWT].astype(jnp.float32) * scale
        held[:, t * 128 : (t + 1) * 128] = part.reshape(ROWT * 16, 128)
    gin_ref[...] = held[0:chan, 0:hid]
    gout_ref[...] = held[0:chan, SIDE : SIDE + hid]
    base = SIDE - 128
    flipped = held[:, base:SIDE].T
    row = hid + KW * KW - base
    gker_ref[...] = flipped[hid - base : row, 0:chan]
    ggain_ref[...] = flipped[row : row + 1, 0:chan]


def greet(devices):
    barrier = pltpu.get_barrier_semaphore()
    for device in devices:
        pl.semaphore_signal(barrier, inc=1, device_id=device, device_id_type=pl.DeviceIdType.MESH)
    pl.semaphore_wait(barrier, len(devices))


def gather_kernel(with_lon, src, side, out, out_side, send_sem, recv_sem, own_sem):
    lat, lon = lax.axis_index("lat"), lax.axis_index("lon")
    z, x, core = lat // 4, (lat // 2) % 2, lat % 2

    def place(step):
        dz, dx, dc = step
        return ((z + dz) % 4) * 4 + ((x + dx) % 2) * 2 + (core + dc) % 2

    def device_of(step):
        return {"lat": place(step), "lon": lon}

    across = {"lat": lat, "lon": (lon + 1) % 2}
    peers = [device_of(p) for p in ((1, 0, 0), (2, 0, 0), (3, 0, 0), (0, 1, 0), (0, 0, 1))]
    greet(peers + [across] * with_lon)
    copies = {}

    def start(key, here, there, n, device):
        copy = pltpu.make_async_remote_copy(
            src_ref=here, dst_ref=there, send_sem=send_sem.at[n], recv_sem=recv_sem.at[n],
            device_id=device, device_id_type=pl.DeviceIdType.MESH,
        )
        copy.start()
        copies[key] = copy

    def send(which, block, hop, landed):
        target = out_side if which else out
        here = target.at[place(block)]
        if which == 0 and block == (0, 0, 0):
            here = src
        dz, dx, dc = landed
        n = which * 16 + (dz * 2 + dx) * 2 + dc
        start((which, landed), here, target.at[place(block)], n, device_of(hop))

    def forward(which, block):
        dz, dx, dc = block
        if dx == 0:
            send(which, block, (0, 1, 0), (dz, 1, 0))
        send(which, block, (0, 0, 1), (dz, dx, 1))

    def spread(which):
        for dz in (2, 1, 3):
            send(which, (0, 0, 0), (dz, 0, 0), ((4 - dz) % 4, 0, 0))
        forward(which, (0, 0, 0))

    if with_lon:
        start("side", side, out_side.at[lat], 32, across)
    spread(0)
    own = pltpu.make_async_copy(src, out.at[lat], own_sem)
    own.start()
    if with_lon:
        copies["side"].wait_recv()
        spread(1)
    kinds = (0, 1) if with_lon else (0,)
    for dz, dx in ((0, 1), (1, 0), (3, 0), (1, 1), (3, 1), (2, 0), (2, 1)):
        for which in kinds:
            copies[which, (dz, dx, 0)].wait_recv()
            forward(which, (dz, dx, 0))
    for which in kinds:
        for dz in range(4):
            for dx in range(2):
                copies[which, (dz, dx, 1)].wait_recv()
    for copy in copies.values():
        copy.wait_send()
    own.wait()


def reduce_kernel(n_lon, per, src, out, first, acc, second, third, sems):
    lat, lon = lax.axis_index("lat"), lax.axis_index("lon")
    z = lat // 4
    groups, deep = n_lon * 4, 4
    span = per * deep
    mine = lon * 4 + lat % 4

    def in_plane(d):
        g = (mine + d) % groups
        return g, {"lat": z * 4 + g % 4, "lon": g // 4}

    def along(d):
        other = (z + d) % deep
        return other, {"lat": other * 4 + lat % 4, "lon": lon}

    greet([in_plane(d)[1] for d in range(1, groups)] + [along(d)[1] for d in range(1, deep)])
    copies = []

    def send(stage, back, here, there, device):
        copy = pltpu.make_async_remote_copy(
            src_ref=here, dst_ref=there, send_sem=sems.at[stage, 0, back], recv_sem=sems.at[stage, 1, back],
            device_id=device, device_id_type=pl.DeviceIdType.MESH,
        )
        copy.start()
        copies.append(copy)
        return copy

    landing = []
    for d in range(1, groups):
        g, device = in_plane(d)
        landing.append(send(0, groups - d, src.at[pl.ds(g * span, span)], first.at[groups - d], device))
    acc[...] = src[pl.ds(mine * span, span)].astype(jnp.float32)
    for d in range(1, groups):
        landing[d - 1].wait_recv()
        acc[...] += first[groups - d].astype(jnp.float32)
    second[...] = acc[...].astype(jnp.bfloat16)
    landing = []
    for d in range(1, deep):
        other, device = along(d)
        landing.append(send(1, deep - d, second.at[pl.ds(other * per, per)], third.at[deep - d], device))
    total = acc[pl.ds(z * per, per)]
    for d in range(1, deep):
        landing[d - 1].wait_recv()
        total += third[deep - d].astype(jnp.float32)
    mark = pl.ds(mine * span + z * per, per)
    out[mark] = total.astype(jnp.bfloat16)
    landing = []
    for d in range(1, deep):
        landing.append(send(2, deep - d, out.at[mark], out.at[mark], along(d)[1]))
    for copy in landing:
        copy.wait_recv()
    whole = pl.ds(mine * span, span)
    landing = []
    for d in range(1, groups):
        landing.append(send(3, groups - d, out.at[whole], out.at[whole], in_plane(d)[1]))
    for copy in landing:
        copy.wait_recv()
    for copy in copies:
        copy.wait_send()


def body(x_tiles, tile_pos, valid_rows, stem_w, dw_kernel, norm_gain, w_in, w_out, cotangent):
    f32 = jnp.float32
    bf16 = jnp.bfloat16
    lat_count = lax.axis_size("lat")
    lon_count = lax.axis_size("lon")
    inputs, places, rows, upstream = x_tiles[0], tile_pos[0], valid_rows[0], cotangent[0]
    tile_count, cin, _ = inputs.shape
    chan, hid = w_in.shape
    lanes = tile_count * EDGE
    smem = pl.BlockSpec(memory_space=pltpu.SMEM)
    vmem = pl.BlockSpec(memory_space=pltpu.VMEM)
    params = pltpu.CompilerParams(vmem_limit_bytes=VMEM_LIMIT)
    side_lanes = tile_count * SIDE_CELLS
    packed, packed_side = pl.pallas_call(
        pack_kernel,
        out_shape=[
            jax.ShapeDtypeStruct((CINP, lanes), bf16),
            jax.ShapeDtypeStruct((CINP, side_lanes), bf16),
        ],
        in_specs=[smem, smem, vmem, vmem, vmem],
        out_specs=[vmem, vmem],
        scratch_shapes=[pltpu.VMEM((CINP, lanes), f32), pltpu.VMEM((CINP, side_lanes), f32)],
        compiler_params=params,
    )(places, rows, inputs, jnp.asarray(edge_pick(), bf16), jnp.asarray(side_pick(), bf16))
    with_lon = lon_count == 2
    gathered, sides = pl.pallas_call(
        functools.partial(gather_kernel, with_lon),
        out_shape=[
            jax.ShapeDtypeStruct((lat_count, CINP, lanes), bf16),
            jax.ShapeDtypeStruct((lat_count, CINP, side_lanes), bf16),
        ],
        in_specs=[vmem, vmem],
        out_specs=[vmem, vmem],
        scratch_shapes=[
            pltpu.SemaphoreType.DMA((33,)),
            pltpu.SemaphoreType.DMA((33,)),
            pltpu.SemaphoreType.DMA,
        ],
        compiler_params=pltpu.CompilerParams(
            vmem_limit_bytes=VMEM_LIMIT, collective_id=0, has_side_effects=True
        ),
    )(packed, packed_side)
    if not with_lon:
        gathered = lax.all_gather(gathered, "lon", tiled=True)

    def described(blocks):
        meta = blocks[:, 77:80, 0:tile_count].astype(f32)
        return (meta[:, 0, :] * 16.0 + meta[:, 1, :]).astype(jnp.int32), jnp.sum(meta[:, 2, :])

    def found(want, keys):
        numbers = np.arange(keys.shape[0] * tile_count, dtype=np.int32)
        codes = jnp.asarray(numbers // tile_count * 8 + numbers % tile_count)
        hit = want[:, :, None] == keys.reshape(-1)[None, None, :]
        return 7 + jnp.sum(jnp.where(hit, codes - 7, 0), axis=2)

    off = np.array(OFFSETS, np.int32)
    want_row = (places >> 3)[:, None] + off[None, :, 0]
    want_col = (places & 7)[:, None] + off[None, :, 1]
    all_place, ocean_rows = described(gathered)
    if with_lon:
        side_place, side_rows = described(sides)
        cell_total = TS * (ocean_rows + side_rows)
        inside = (want_col >= 0) & (want_col < TCOLS)
        want = want_row * TCOLS + (want_col & 7)
        near = jnp.concatenate(
            [
                found(jnp.where(inside, want, -1), all_place),
                found(jnp.where(inside, -1, want), side_place),
            ],
            axis=1,
        )
    else:
        cell_total = TS * ocean_rows
        around = TCOLS * lon_count
        sector = jnp.arange(lon_count * lat_count, dtype=jnp.int32)[:, None] // lat_count
        keys = (all_place >> 3) * around + sector * TCOLS + (all_place & 7)
        want_col = (want_col + lax.axis_index("lon") * TCOLS) % around
        near = found(want_row * around + want_col, keys)
    pick = halo_pick(with_lon)
    groups = lon_count * 4
    per = -(-USED // (groups * 4))
    tiles_all = per * groups * 4
    result, packed_sums = pl.pallas_call(
        functools.partial(block_kernel, with_lon),
        out_shape=[
            jax.ShapeDtypeStruct((tile_count, chan, CELLS), bf16),
            jax.ShapeDtypeStruct((tiles_all, 16, 128), bf16),
        ],
        in_specs=[smem, smem] + [vmem] * 10,
        out_specs=[vmem] * 2,
        scratch_shapes=[
            pltpu.VMEM((ROWT * 16, WIDE), f32),
            pltpu.VMEM((128, 256), f32),
            pltpu.VMEM((CINP, chan), bf16),
            pltpu.VMEM((tile_count, CINP, pick.shape[0]), bf16),
            pltpu.VMEM((tile_count, CINP, PR * PC), f32),
            pltpu.VMEM((PR, PC, chan), f32),
            pltpu.VMEM((TS, TS, chan), f32),
            pltpu.VMEM((TS, TS, 128), f32),
            pltpu.VMEM((tile_count * CELLS, chan), bf16),
            pltpu.VMEM((tile_count * CELLS, hid), bf16),
            pltpu.VMEM((tile_count * CELLS, hid), bf16),
            pltpu.VMEM((tile_count, chan, CELLS), bf16),
            pltpu.VMEM((TS, TS, chan), f32),
            pltpu.VMEM((KW * KW, 8, chan), f32),
            pltpu.VMEM((8, chan), f32),
        ],
        compiler_params=params,
    )(
        near, rows, gathered, sides, inputs, upstream, jnp.asarray(pick, bf16),
        stem_w, dw_kernel.T, norm_gain[None], w_in, w_out.T,
    )
    span = per * 4
    reduced = pl.pallas_call(
        functools.partial(reduce_kernel, lon_count, per),
        out_shape=jax.ShapeDtypeStruct((tiles_all, 16, 128), bf16),
        in_specs=[vmem],
        out_specs=vmem,
        scratch_shapes=[
            pltpu.VMEM((groups, span, 16, 128), bf16),
            pltpu.VMEM((span, 16, 128), f32),
            pltpu.VMEM((span, 16, 128), bf16),
            pltpu.VMEM((4, per, 16, 128), bf16),
            pltpu.SemaphoreType.DMA((4, 2, groups)),
        ],
        compiler_params=pltpu.CompilerParams(
            vmem_limit_bytes=VMEM_LIMIT, collective_id=1, has_side_effects=True
        ),
    )(packed_sums)
    sum_in, sum_out, sum_kernel, sum_gain = pl.pallas_call(
        unpack_kernel,
        out_shape=[
            jax.ShapeDtypeStruct((chan, hid), f32),
            jax.ShapeDtypeStruct((chan, hid), f32),
            jax.ShapeDtypeStruct((KW * KW, chan), f32),
            jax.ShapeDtypeStruct((1, chan), f32),
        ],
        in_specs=[smem, vmem],
        out_specs=[vmem] * 4,
        scratch_shapes=[pltpu.VMEM((ROWT * 16, WIDE), f32)],
        compiler_params=params,
    )(cell_total.reshape(1), reduced)
    return result[None], sum_in, sum_out.T, sum_kernel.T, sum_gain[0]


def solution(mesh):
    in_specs = (
        P("lon", "lat", None, None),
        P("lon", "lat"),
        P("lon", "lat"),
        P(),
        P(),
        P(),
        P(),
        P(),
        P("lon", "lat", None, None),
    )
    out_specs = (P("lon", "lat", None, None), P(), P(), P(), P())
    return jax.shard_map(body, mesh=mesh, in_specs=in_specs, out_specs=out_specs, check_vma=False)
```

```python
import functools

import jax
import jax.numpy as jnp
import numpy as np
from jax import lax
from jax.experimental import pallas as pl
from jax.experimental.pallas import tpu as pltpu
from jax.sharding import PartitionSpec as P

TS = 16
CELLS = TS * TS
KW = 7
REACH = KW // 2
TCOLS = 8
EDGE = 160
PR = TS + 2 * REACH
PC = 24
CINP = 80
SIDE_CELLS = 64
SLAB = 128
REST = EDGE - SLAB
KROWS = CELLS + 9 * SLAB
OFFSETS = ((-1, -1), (-1, 0), (-1, 1), (0, -1), (0, 1), (1, -1), (1, 0), (1, 1))
SIDE = 896
WIDE = 2 * SIDE
ROWT = 13
USED = ROWT * WIDE // 128
VMEM_LIMIT = 56 * 1024 * 1024


def edge_lane(y, x):
    low, high = REACH, TS - REACH
    if x < low:
        return y * REACH + x
    if x >= high:
        return SIDE_CELLS + y * REACH + x - high
    if y < low:
        middle = y * (high - low) + x - low
        return 48 + middle if middle < 16 else 96 + middle
    if y >= high:
        return SLAB + (y - high) * (high - low) + x - low
    return -1


def edge_pick():
    pick = np.zeros((CELLS, EDGE), np.float32)
    for y in range(TS):
        for x in range(TS):
            if edge_lane(y, x) >= 0:
                pick[y * TS + x, edge_lane(y, x)] = 1
    return pick


def side_pick():
    pick = np.zeros((2, CELLS, SIDE_CELLS), np.float32)
    for y in range(TS):
        for x in range(REACH):
            pick[0, y * TS + x, y * REACH + x] = 1
            pick[1, y * TS + TS - REACH + x, y * REACH + x] = 1
    return pick


def halo_pick(tile_count):
    pick = np.zeros((KROWS, PR * PC), np.float32)
    for py in range(PR):
        for px in range(PR):
            y, x = py - REACH, px - REACH
            dy, dx = y // TS, x // TS
            cell = py * PC + px
            if (dy, dx) == (0, 0):
                pick[y * TS + x, cell] = 1
                continue
            lane = edge_lane(y % TS, x % TS)
            if lane < SLAB:
                pick[CELLS + OFFSETS.index((dy, dx)) * SLAB + lane, cell] = 1
            else:
                for a in range(tile_count):
                    pick[CELLS + 8 * SLAB + a * REST + lane - SLAB, cell] = 1
    return pick


def pack_kernel(places, rows, x_ref, pick_ref, side_ref, out_ref, out_side_ref, held, held_side):
    tile_count, cin, _ = x_ref.shape
    cell_row = lax.broadcasted_iota(jnp.int32, (1, CELLS), 1) // TS
    held[...] = jnp.zeros_like(held)
    held_side[...] = jnp.zeros_like(held_side)
    for a in range(tile_count):
        keep = (cell_row < rows[a]).astype(jnp.float32)
        tile = (x_ref[a].astype(jnp.float32) * keep).astype(jnp.bfloat16)
        edges = jnp.dot(tile, pick_ref[...], preferred_element_type=jnp.float32)
        held[0:cin, a * SLAB : (a + 1) * SLAB] = edges[:, 0:SLAB]
        base = tile_count * SLAB + a * REST
        held[0:cin, base : base + REST] = edges[:, SLAB:EDGE]
        outer = jnp.where((places[a] & (TCOLS - 1)) == 0, side_ref[0], side_ref[1])
        held_side[0:cin, a * SIDE_CELLS : (a + 1) * SIDE_CELLS] = jnp.dot(
            tile, outer, preferred_element_type=jnp.float32
        )
    owner = lax.broadcasted_iota(jnp.int32, (1, 128), 1)
    high = jnp.zeros((1, 128), jnp.int32)
    low = jnp.zeros((1, 128), jnp.int32)
    ocean = jnp.zeros((1, 128), jnp.int32)
    for a in range(tile_count):
        high = jnp.where(owner == a, places[a] >> 4, high)
        low = jnp.where(owner == a, places[a] & 15, low)
        ocean = jnp.where(owner == a, rows[a], ocean)
    for target in (held, held_side):
        target[77:78, 0:128] = high.astype(jnp.float32)
        target[78:79, 0:128] = low.astype(jnp.float32)
        target[79:80, 0:128] = ocean.astype(jnp.float32)
    out_ref[...] = held[...].astype(jnp.bfloat16)
    out_side_ref[...] = held_side[...].astype(jnp.bfloat16)


def block_kernel(
    with_lon, near, rows, gathered, sides, x_ref, cot_ref, pick_ref, stem_ref, taps_ref, gain_ref, win_ref, wout_ref,
    out_ref, pack_ref,
    held, small, stem_s, sources, raw, padded, unit_s, inv_s, feats, hiddens, gpres, grads_t, gconv, kacc, gacc,
):
    f32 = jnp.float32
    bf16 = jnp.bfloat16
    tile_count, cin, _ = x_ref.shape
    chan = cot_ref.shape[1]
    lane_row = lax.broadcasted_iota(jnp.int32, (1, CELLS), 1) // TS
    kacc[...] = jnp.zeros_like(kacc)
    gacc[...] = jnp.zeros_like(gacc)
    sources[...] = jnp.zeros_like(sources)
    stem_s[...] = jnp.zeros_like(stem_s)
    stem_s[0:cin, :] = stem_ref[...]

    for a in range(tile_count):
        keep = (lane_row < rows[a]).astype(f32)
        tile = (x_ref[a].astype(f32) * keep).astype(bf16)
        sources[a, 0:cin, 0:CELLS] = tile
        for n, (dy, dx) in enumerate(OFFSETS):
            code = near[a, n]
            slot = code & 7
            from_lane = pl.multiple_of((slot & 3) * SLAB, SLAB)
            piece = gathered[code >> 3, :, pl.ds(from_lane, SLAB)]
            piece = jnp.where(slot < tile_count, piece, jnp.zeros_like(piece))
            if with_lon and dx != 0:
                other = near[a, 8 + n]
                spot = other & 7
                from_lane = pl.multiple_of(((spot & 3) >> 1) * SLAB, SLAB)
                outer = sides[other >> 3, :, pl.ds(from_lane, SLAB)]
                turned = jnp.concatenate([outer[:, SIDE_CELLS:], outer[:, :SIDE_CELLS]], axis=1)
                outer = jnp.where((spot & 1) == (0 if dx > 0 else 1), outer, turned)
                piece = jnp.where(spot < tile_count, outer, piece)
            sources[a, :, CELLS + n * SLAB : CELLS + (n + 1) * SLAB] = piece
            if (dy, dx) == (-1, 0):
                rest = gathered[code >> 3, :, tile_count * SLAB : tile_count * EDGE]
                rest_of = lax.broadcasted_iota(jnp.int32, rest.shape, 1) // REST
                sources[a, :, CELLS + 8 * SLAB :] = (
                    rest.astype(f32) * (rest_of == slot).astype(f32)
                ).astype(bf16)
    raw[...] = jnp.dot(
        sources[...].reshape(tile_count * CINP, pick_ref.shape[0]), pick_ref[...], preferred_element_type=f32
    ).reshape(tile_count, CINP, PR * PC)

    @pl.loop(0, tile_count)
    def _(a):
        cells_in = raw[a].T.astype(bf16)
        stems = jnp.dot(cells_in, stem_s[...], preferred_element_type=f32)
        padded[...] = stems.astype(bf16).astype(f32).reshape(PR, PC, chan)

        @pl.loop(0, TS // 4)
        def _(yb):
            y0 = yb * 4
            acc = jnp.zeros((4, TS, chan), f32)
            for k in range(KW):
                shifted = padded[pl.ds(y0, 4 + KW - 1), k : k + TS, :]
                for r in range(KW):
                    acc += taps_ref[r * KW + k : r * KW + k + 1, :][None] * shifted[r : r + 4]
            mean = jnp.mean(acc, axis=2, keepdims=True)
            centred = acc - mean
            inv = lax.rsqrt(jnp.mean(centred * centred, axis=2, keepdims=True) + 1e-06)
            unit_s[pl.ds(y0, 4)] = centred * inv
            inv_s[pl.ds(y0, 4)] = jnp.broadcast_to(inv, (4, TS, 128))

        gain = gain_ref[...]
        unit = unit_s[...].reshape(CELLS, chan)
        feat = (unit * gain).astype(bf16)
        feats[pl.ds(a * CELLS, CELLS), :] = feat
        pre = jnp.dot(feat, win_ref[...], preferred_element_type=f32)
        keep = (lane_row < rows[a]).astype(f32)
        mgrad_t = (cot_ref[a].astype(f32) * keep).astype(bf16)
        grads_t[a] = mgrad_t
        mgrad = mgrad_t.astype(f32).T.astype(bf16)
        ghid = jnp.dot(mgrad, wout_ref[...], preferred_element_type=f32)
        square = pre * pre
        bend = jnp.tanh(0.7978845608028654 * pre * (1.0 + 0.044715 * square))
        half = 0.5 * (1.0 + bend)
        hidden = (pre * half).astype(bf16)
        slope = half + 0.5 * pre * (1.0 - bend * bend) * (0.7978845608028654 * (1.0 + 0.134145 * square))
        gpre = (ghid * slope).astype(bf16)
        hiddens[pl.ds(a * CELLS, CELLS), :] = hidden
        gpres[pl.ds(a * CELLS, CELLS), :] = gpre
        branch = lax.dot_general(
            hidden, wout_ref[...], (((1,), (1,)), ((), ())), preferred_element_type=f32
        )
        stem_own = padded[REACH : REACH + TS, REACH : REACH + TS, :].reshape(CELLS, chan)
        out_ref[a] = ((stem_own + branch).T * keep).astype(bf16)
        gfeat = lax.dot_general(gpre, win_ref[...], (((1,), (1,)), ((), ())), preferred_element_type=f32)
        gfeat = gfeat.astype(bf16).astype(f32)
        gacc[...] += jnp.sum((gfeat * unit).reshape(CELLS // 8, 8, chan), axis=0)
        scaled = gfeat * gain
        first = jnp.mean(scaled, axis=1, keepdims=True)
        second = jnp.mean(scaled * unit, axis=1, keepdims=True)
        inv = inv_s[...].reshape(CELLS, 128)[:, 0:1]
        gconv[...] = (inv * (scaled - first - unit * second)).reshape(TS, TS, chan)

        @pl.loop(0, TS // 4)
        def _(yb):
            y0 = yb * 4
            grad = gconv[pl.ds(y0, 4)]
            for k in range(KW):
                shifted = padded[pl.ds(y0, 4 + KW - 1), k : k + TS, :]
                for r in range(KW):
                    prod = grad * shifted[r : r + 4]
                    kacc[r * KW + k] += jnp.sum(prod.reshape(8, 8, chan), axis=0)

    held[...] = jnp.zeros_like(held)
    small[...] = jnp.zeros_like(small)
    hid = win_ref.shape[1]
    held[0:chan, 0:hid] = lax.dot_general(
        feats[...], gpres[...], (((0,), (0,)), ((), ())), preferred_element_type=f32
    )
    total = jnp.zeros((chan, hid), f32)
    for a in range(tile_count):
        total += jnp.dot(grads_t[a], hiddens[a * CELLS : (a + 1) * CELLS, :], preferred_element_type=f32)
    held[0:chan, SIDE : SIDE + hid] = total
    small[0 : KW * KW, 0:chan] = jnp.sum(kacc[...], axis=1)
    small[KW * KW : KW * KW + 1, 0:chan] = jnp.sum(gacc[...], axis=0, keepdims=True)
    held[0:chan, hid:SIDE] = small[...].T[0:chan, 0 : SIDE - hid]
    for t in range(WIDE // 128):
        part = held[:, t * 128 : (t + 1) * 128].astype(bf16)
        pack_ref[t * ROWT : (t + 1) * ROWT] = part.reshape(ROWT, 16, 128)
    spare = pack_ref.shape[0] - USED
    pack_ref[USED:] = jnp.zeros((spare, 16, 128), bf16)


def unpack_kernel(total_ref, tiles_ref, gin_ref, gout_ref, gker_ref, ggain_ref, held):
    scale = 1.0 / total_ref[0]
    chan, hid = gin_ref.shape
    for t in range(WIDE // 128):
        part = tiles_ref[t * ROWT : (t + 1) * ROWT].astype(jnp.float32) * scale
        held[:, t * 128 : (t + 1) * 128] = part.reshape(ROWT * 16, 128)
    gin_ref[...] = held[0:chan, 0:hid]
    gout_ref[...] = held[0:chan, SIDE : SIDE + hid]
    base = SIDE - 128
    flipped = held[:, base:SIDE].T
    row = hid + KW * KW - base
    gker_ref[...] = flipped[hid - base : row, 0:chan]
    ggain_ref[...] = flipped[row : row + 1, 0:chan]


def greet(devices):
    barrier = pltpu.get_barrier_semaphore()
    for device in devices:
        pl.semaphore_signal(barrier, inc=1, device_id=device, device_id_type=pl.DeviceIdType.MESH)
    pl.semaphore_wait(barrier, len(devices))


def gather_kernel(with_lon, src, side, out, out_side, send_sem, recv_sem, own_sem):
    lat, lon = lax.axis_index("lat"), lax.axis_index("lon")
    z, x, core = lat // 4, (lat // 2) % 2, lat % 2

    def place(step):
        dz, dx, dc = step
        return ((z + dz) % 4) * 4 + ((x + dx) % 2) * 2 + (core + dc) % 2

    def device_of(step):
        return {"lat": place(step), "lon": lon}

    across = {"lat": lat, "lon": (lon + 1) % 2}
    peers = [device_of(p) for p in ((1, 0, 0), (2, 0, 0), (3, 0, 0), (0, 1, 0), (0, 0, 1))]
    greet(peers + [across] * with_lon)
    copies = {}

    def start(key, here, there, n, device):
        copy = pltpu.make_async_remote_copy(
            src_ref=here, dst_ref=there, send_sem=send_sem.at[n], recv_sem=recv_sem.at[n],
            device_id=device, device_id_type=pl.DeviceIdType.MESH,
        )
        copy.start()
        copies[key] = copy

    def send(which, block, hop, landed):
        target = out_side if which else out
        here = target.at[place(block)]
        if which == 0 and block == (0, 0, 0):
            here = src
        dz, dx, dc = landed
        n = which * 16 + (dz * 2 + dx) * 2 + dc
        start((which, landed), here, target.at[place(block)], n, device_of(hop))

    def forward(which, block):
        dz, dx, dc = block
        if dx == 0:
            send(which, block, (0, 1, 0), (dz, 1, 0))
        send(which, block, (0, 0, 1), (dz, dx, 1))

    def spread(which):
        for dz in (2, 1, 3):
            send(which, (0, 0, 0), (dz, 0, 0), ((4 - dz) % 4, 0, 0))
        forward(which, (0, 0, 0))

    if with_lon:
        start("side", side, out_side.at[lat], 32, across)
    spread(0)
    own = pltpu.make_async_copy(src, out.at[lat], own_sem)
    own.start()
    if with_lon:
        copies["side"].wait_recv()
        spread(1)
    kinds = (0, 1) if with_lon else (0,)
    for dz, dx in ((0, 1), (1, 0), (3, 0), (1, 1), (3, 1), (2, 0), (2, 1)):
        for which in kinds:
            copies[which, (dz, dx, 0)].wait_recv()
            forward(which, (dz, dx, 0))
    for which in kinds:
        for dz in range(4):
            for dx in range(2):
                copies[which, (dz, dx, 1)].wait_recv()
    for copy in copies.values():
        copy.wait_send()
    own.wait()


def reduce_kernel(n_lon, per, src, out, first, middle, second, acc, fourth, third, sems):
    lat, lon = lax.axis_index("lat"), lax.axis_index("lon")
    z, x, core = lat // 4, (lat // 2) % 2, lat % 2
    chips, deep = n_lon * 2, 4
    span = per * deep

    def chip(d):
        return (lon * 2 + x + d) % chips

    def device_at(d):
        q = chip(d)
        return {"lat": z * 4 + (q % 2) * 2 + core, "lon": q // 2}

    def along(d):
        other = (z + d) % deep
        return other, {"lat": other * 4 + lat % 4, "lon": lon}

    def region(d, half):
        return pl.ds((chip(d) * 2 + half) * span, span)

    partner = {"lat": z * 4 + x * 2 + 1 - core, "lon": lon}
    greet(
        [partner]
        + [device_at(d) for d in range(1, chips)]
        + [along(d)[1] for d in range(1, deep)]
    )
    copies = []

    def send(stage, back, here, there, device):
        copy = pltpu.make_async_remote_copy(
            src_ref=here, dst_ref=there, send_sem=sems.at[stage, 0, back], recv_sem=sems.at[stage, 1, back],
            device_id=device, device_id_type=pl.DeviceIdType.MESH,
        )
        copy.start()
        copies.append(copy)
        return copy

    f32, bf16 = jnp.float32, jnp.bfloat16
    order = list(range(1, chips)) + [0]
    halves = {}
    for d in order:
        halves[d] = send(0, d, src.at[region(d, 1 - core)], first.at[d], partner)
    landing = []
    for d in order:
        halves[d].wait_recv()
        pair = src[region(d, core)].astype(f32) + first[d].astype(f32)
        if d == 0:
            acc[...] = pair
        else:
            middle[d] = pair.astype(bf16)
            landing.append(send(1, chips - d, middle.at[d], second.at[chips - d], device_at(d)))
    for d in range(1, chips):
        landing[d - 1].wait_recv()
        acc[...] += second[chips - d].astype(f32)
    fourth[...] = acc[...].astype(bf16)
    landing = []
    for d in range(1, deep):
        other, device = along(d)
        landing.append(send(2, deep - d, fourth.at[pl.ds(other * per, per)], third.at[deep - d], device))
    total = acc[pl.ds(z * per, per)]
    for d in range(1, deep):
        landing[d - 1].wait_recv()
        total += third[deep - d].astype(f32)
    mark = pl.ds((chip(0) * 2 + core) * span + z * per, per)
    out[mark] = total.astype(bf16)
    landing = []
    for d in range(1, deep):
        landing.append(send(3, deep - d, out.at[mark], out.at[mark], along(d)[1]))
    for copy in landing:
        copy.wait_recv()
    whole = region(0, core)
    landing = []
    for d in range(1, chips):
        landing.append(send(4, chips - d, out.at[whole], out.at[whole], device_at(d)))
    final = [send(5, 0, out.at[whole], out.at[whole], partner)]
    for d in range(1, chips):
        landing[d - 1].wait_recv()
        came = region(chips - d, core)
        final.append(send(5, chips - d, out.at[came], out.at[came], partner))
    for copy in final:
        copy.wait_recv()
    for copy in copies:
        copy.wait_send()


def body(x_tiles, tile_pos, valid_rows, stem_w, dw_kernel, norm_gain, w_in, w_out, cotangent):
    f32 = jnp.float32
    bf16 = jnp.bfloat16
    lat_count = lax.axis_size("lat")
    lon_count = lax.axis_size("lon")
    inputs, places, rows, upstream = x_tiles[0], tile_pos[0], valid_rows[0], cotangent[0]
    tile_count, cin, _ = inputs.shape
    chan, hid = w_in.shape
    lanes = tile_count * EDGE
    smem = pl.BlockSpec(memory_space=pltpu.SMEM)
    vmem = pl.BlockSpec(memory_space=pltpu.VMEM)
    params = pltpu.CompilerParams(vmem_limit_bytes=VMEM_LIMIT)
    side_lanes = tile_count * SIDE_CELLS
    packed, packed_side = pl.pallas_call(
        pack_kernel,
        out_shape=[
            jax.ShapeDtypeStruct((CINP, lanes), bf16),
            jax.ShapeDtypeStruct((CINP, side_lanes), bf16),
        ],
        in_specs=[smem, smem, vmem, vmem, vmem],
        out_specs=[vmem, vmem],
        scratch_shapes=[pltpu.VMEM((CINP, lanes), f32), pltpu.VMEM((CINP, side_lanes), f32)],
        compiler_params=params,
    )(places, rows, inputs, jnp.asarray(edge_pick(), bf16), jnp.asarray(side_pick(), bf16))
    with_lon = lon_count == 2
    gathered, sides = pl.pallas_call(
        functools.partial(gather_kernel, with_lon),
        out_shape=[
            jax.ShapeDtypeStruct((lat_count, CINP, lanes), bf16),
            jax.ShapeDtypeStruct((lat_count, CINP, side_lanes), bf16),
        ],
        in_specs=[vmem, vmem],
        out_specs=[vmem, vmem],
        scratch_shapes=[
            pltpu.SemaphoreType.DMA((33,)),
            pltpu.SemaphoreType.DMA((33,)),
            pltpu.SemaphoreType.DMA,
        ],
        compiler_params=pltpu.CompilerParams(
            vmem_limit_bytes=VMEM_LIMIT, collective_id=0, has_side_effects=True
        ),
    )(packed, packed_side)
    if not with_lon:
        gathered = lax.all_gather(gathered, "lon", tiled=True)

    def described(blocks):
        meta = blocks[:, 77:80, 0:tile_count].astype(f32)
        return (meta[:, 0, :] * 16.0 + meta[:, 1, :]).astype(jnp.int32), jnp.sum(meta[:, 2, :])

    def found(want, keys):
        numbers = np.arange(keys.shape[0] * tile_count, dtype=np.int32)
        codes = jnp.asarray(numbers // tile_count * 8 + numbers % tile_count)
        hit = want[:, :, None] == keys.reshape(-1)[None, None, :]
        return 7 + jnp.sum(jnp.where(hit, codes - 7, 0), axis=2)

    off = np.array(OFFSETS, np.int32)
    want_row = (places >> 3)[:, None] + off[None, :, 0]
    want_col = (places & 7)[:, None] + off[None, :, 1]
    all_place, ocean_rows = described(gathered)
    if with_lon:
        side_place, side_rows = described(sides)
        cell_total = TS * (ocean_rows + side_rows)
        inside = (want_col >= 0) & (want_col < TCOLS)
        want = want_row * TCOLS + (want_col & 7)
        near = jnp.concatenate(
            [
                found(jnp.where(inside, want, -1), all_place),
                found(jnp.where(inside, -1, want), side_place),
            ],
            axis=1,
        )
    else:
        cell_total = TS * ocean_rows
        around = TCOLS * lon_count
        sector = jnp.arange(lon_count * lat_count, dtype=jnp.int32)[:, None] // lat_count
        keys = (all_place >> 3) * around + sector * TCOLS + (all_place & 7)
        want_col = (want_col + lax.axis_index("lon") * TCOLS) % around
        near = found(want_row * around + want_col, keys)
    pick = halo_pick(tile_count)
    groups = lon_count * 4
    per = -(-USED // (groups * 4))
    tiles_all = per * groups * 4
    result, packed_sums = pl.pallas_call(
        functools.partial(block_kernel, with_lon),
        out_shape=[
            jax.ShapeDtypeStruct((tile_count, chan, CELLS), bf16),
            jax.ShapeDtypeStruct((tiles_all, 16, 128), bf16),
        ],
        in_specs=[smem, smem] + [vmem] * 10,
        out_specs=[vmem] * 2,
        scratch_shapes=[
            pltpu.VMEM((ROWT * 16, WIDE), f32),
            pltpu.VMEM((128, 256), f32),
            pltpu.VMEM((CINP, chan), bf16),
            pltpu.VMEM((tile_count, CINP, pick.shape[0]), bf16),
            pltpu.VMEM((tile_count, CINP, PR * PC), f32),
            pltpu.VMEM((PR, PC, chan), f32),
            pltpu.VMEM((TS, TS, chan), f32),
            pltpu.VMEM((TS, TS, 128), f32),
            pltpu.VMEM((tile_count * CELLS, chan), bf16),
            pltpu.VMEM((tile_count * CELLS, hid), bf16),
            pltpu.VMEM((tile_count * CELLS, hid), bf16),
            pltpu.VMEM((tile_count, chan, CELLS), bf16),
            pltpu.VMEM((TS, TS, chan), f32),
            pltpu.VMEM((KW * KW, 8, chan), f32),
            pltpu.VMEM((8, chan), f32),
        ],
        compiler_params=params,
    )(
        near, rows, gathered, sides, inputs, upstream, jnp.asarray(pick, bf16),
        stem_w, dw_kernel.T, norm_gain[None], w_in, w_out.T,
    )
    span = per * 4
    chips = lon_count * 2
    reduced = pl.pallas_call(
        functools.partial(reduce_kernel, lon_count, per),
        out_shape=jax.ShapeDtypeStruct((tiles_all, 16, 128), bf16),
        in_specs=[vmem],
        out_specs=vmem,
        scratch_shapes=[
            pltpu.VMEM((chips, span, 16, 128), bf16),
            pltpu.VMEM((chips, span, 16, 128), bf16),
            pltpu.VMEM((chips, span, 16, 128), bf16),
            pltpu.VMEM((span, 16, 128), f32),
            pltpu.VMEM((span, 16, 128), bf16),
            pltpu.VMEM((4, per, 16, 128), bf16),
            pltpu.SemaphoreType.DMA((6, 2, max(chips, 4))),
        ],
        compiler_params=pltpu.CompilerParams(
            vmem_limit_bytes=VMEM_LIMIT, collective_id=1, has_side_effects=True
        ),
    )(packed_sums)
    sum_in, sum_out, sum_kernel, sum_gain = pl.pallas_call(
        unpack_kernel,
        out_shape=[
            jax.ShapeDtypeStruct((chan, hid), f32),
            jax.ShapeDtypeStruct((chan, hid), f32),
            jax.ShapeDtypeStruct((KW * KW, chan), f32),
            jax.ShapeDtypeStruct((1, chan), f32),
        ],
        in_specs=[smem, vmem],
        out_specs=[vmem] * 4,
        scratch_shapes=[pltpu.VMEM((ROWT * 16, WIDE), f32)],
        compiler_params=params,
    )(cell_total.reshape(1), reduced)
    return result[None], sum_in, sum_out.T, sum_kernel.T, sum_gain[0]


def solution(mesh):
    in_specs = (
        P("lon", "lat", None, None),
        P("lon", "lat"),
        P("lon", "lat"),
        P(),
        P(),
        P(),
        P(),
        P(),
        P("lon", "lat", None, None),
    )
    out_specs = (P("lon", "lat", None, None), P(), P(), P(), P())
    return jax.shard_map(body, mesh=mesh, in_specs=in_specs, out_specs=out_specs, check_vma=False)
```

```python
import functools

import jax
import jax.numpy as jnp
import numpy as np
from jax import lax
from jax.experimental import pallas as pl
from jax.experimental.pallas import tpu as pltpu
from jax.sharding import PartitionSpec as P

TS = 16
CELLS = TS * TS
KW = 7
REACH = KW // 2
TCOLS = 8
EDGE = 160
PR = TS + 2 * REACH
PC = 24
CINP = 80
SIDE_CELLS = 64
SLAB = 128
REST = EDGE - SLAB
KROWS = CELLS + 9 * SLAB
OFFSETS = ((-1, -1), (-1, 0), (-1, 1), (0, -1), (0, 1), (1, -1), (1, 0), (1, 1))
SIDE = 896
WIDE = 2 * SIDE
ROWT = 13
USED = ROWT * WIDE // 128
VMEM_LIMIT = 56 * 1024 * 1024


def edge_lane(y, x):
    low, high = REACH, TS - REACH
    if x < low:
        return y * REACH + x
    if x >= high:
        return SIDE_CELLS + y * REACH + x - high
    if y < low:
        middle = y * (high - low) + x - low
        return 48 + middle if middle < 16 else 96 + middle
    if y >= high:
        return SLAB + (y - high) * (high - low) + x - low
    return -1


def edge_pick():
    pick = np.zeros((CELLS, EDGE), np.float32)
    for y in range(TS):
        for x in range(TS):
            if edge_lane(y, x) >= 0:
                pick[y * TS + x, edge_lane(y, x)] = 1
    return pick


def side_pick():
    pick = np.zeros((2, CELLS, SIDE_CELLS), np.float32)
    for y in range(TS):
        for x in range(REACH):
            pick[0, y * TS + x, y * REACH + x] = 1
            pick[1, y * TS + TS - REACH + x, y * REACH + x] = 1
    return pick


def halo_pick(tile_count):
    pick = np.zeros((KROWS, PR * PC), np.float32)
    for py in range(PR):
        for px in range(PR):
            y, x = py - REACH, px - REACH
            dy, dx = y // TS, x // TS
            cell = py * PC + px
            if (dy, dx) == (0, 0):
                pick[y * TS + x, cell] = 1
                continue
            lane = edge_lane(y % TS, x % TS)
            if lane < SLAB:
                pick[CELLS + OFFSETS.index((dy, dx)) * SLAB + lane, cell] = 1
            else:
                for a in range(tile_count):
                    pick[CELLS + 8 * SLAB + a * REST + lane - SLAB, cell] = 1
    return pick


def pack_kernel(places, rows, x_ref, pick_ref, side_ref, out_ref, out_side_ref, held, held_side):
    tile_count, cin, _ = x_ref.shape
    cell_row = lax.broadcasted_iota(jnp.int32, (1, CELLS), 1) // TS
    held[...] = jnp.zeros_like(held)
    held_side[...] = jnp.zeros_like(held_side)
    for a in range(tile_count):
        keep = (cell_row < rows[a]).astype(jnp.float32)
        tile = (x_ref[a].astype(jnp.float32) * keep).astype(jnp.bfloat16)
        edges = jnp.dot(tile, pick_ref[...], preferred_element_type=jnp.float32)
        held[0:cin, a * SLAB : (a + 1) * SLAB] = edges[:, 0:SLAB]
        base = tile_count * SLAB + a * REST
        held[0:cin, base : base + REST] = edges[:, SLAB:EDGE]
        outer = jnp.where((places[a] & (TCOLS - 1)) == 0, side_ref[0], side_ref[1])
        held_side[0:cin, a * SIDE_CELLS : (a + 1) * SIDE_CELLS] = jnp.dot(
            tile, outer, preferred_element_type=jnp.float32
        )
    owner = lax.broadcasted_iota(jnp.int32, (1, 128), 1)
    high = jnp.zeros((1, 128), jnp.int32)
    low = jnp.zeros((1, 128), jnp.int32)
    ocean = jnp.zeros((1, 128), jnp.int32)
    for a in range(tile_count):
        high = jnp.where(owner == a, places[a] >> 4, high)
        low = jnp.where(owner == a, places[a] & 15, low)
        ocean = jnp.where(owner == a, rows[a], ocean)
    for target in (held, held_side):
        target[77:78, 0:128] = high.astype(jnp.float32)
        target[78:79, 0:128] = low.astype(jnp.float32)
        target[79:80, 0:128] = ocean.astype(jnp.float32)
    out_ref[...] = held[...].astype(jnp.bfloat16)
    out_side_ref[...] = held_side[...].astype(jnp.bfloat16)


def block_kernel(
    with_lon, near, rows, gathered, sides, x_ref, cot_ref, pick_ref, stem_ref, taps_ref, gain_ref, win_ref, wout_ref,
    out_ref, pack_ref,
    held, small, stem_s, sources, raw, padded, unit_s, inv_s, feats, hiddens, gpres, grads_t, gconv, kacc, gacc,
):
    f32 = jnp.float32
    bf16 = jnp.bfloat16
    tile_count, cin, _ = x_ref.shape
    chan = cot_ref.shape[1]
    lane_row = lax.broadcasted_iota(jnp.int32, (1, CELLS), 1) // TS
    kacc[...] = jnp.zeros_like(kacc)
    gacc[...] = jnp.zeros_like(gacc)
    sources[...] = jnp.zeros_like(sources)
    stem_s[...] = jnp.zeros_like(stem_s)
    stem_s[0:cin, :] = stem_ref[...]

    for a in range(tile_count):
        keep = (lane_row < rows[a]).astype(f32)
        tile = (x_ref[a].astype(f32) * keep).astype(bf16)
        sources[a, 0:cin, 0:CELLS] = tile
        for n, (dy, dx) in enumerate(OFFSETS):
            code = near[a, n]
            slot = code & 7
            from_lane = pl.multiple_of((slot & 3) * SLAB, SLAB)
            piece = gathered[code >> 3, :, pl.ds(from_lane, SLAB)]
            piece = jnp.where(slot < tile_count, piece, jnp.zeros_like(piece))
            if with_lon and dx != 0:
                other = near[a, 8 + n]
                spot = other & 7
                from_lane = pl.multiple_of(((spot & 3) >> 1) * SLAB, SLAB)
                outer = sides[other >> 3, :, pl.ds(from_lane, SLAB)]
                turned = jnp.concatenate([outer[:, SIDE_CELLS:], outer[:, :SIDE_CELLS]], axis=1)
                outer = jnp.where((spot & 1) == (0 if dx > 0 else 1), outer, turned)
                piece = jnp.where(spot < tile_count, outer, piece)
            sources[a, :, CELLS + n * SLAB : CELLS + (n + 1) * SLAB] = piece
            if (dy, dx) == (-1, 0):
                rest = gathered[code >> 3, :, tile_count * SLAB : tile_count * EDGE]
                rest_of = lax.broadcasted_iota(jnp.int32, rest.shape, 1) // REST
                sources[a, :, CELLS + 8 * SLAB :] = (
                    rest.astype(f32) * (rest_of == slot).astype(f32)
                ).astype(bf16)
    raw[...] = jnp.dot(
        sources[...].reshape(tile_count * CINP, pick_ref.shape[0]), pick_ref[...], preferred_element_type=f32
    ).reshape(tile_count, CINP, PR * PC)

    @pl.loop(0, tile_count)
    def _(a):
        cells_in = raw[a].T.astype(bf16)
        stems = jnp.dot(cells_in, stem_s[...], preferred_element_type=f32)
        padded[...] = stems.astype(bf16).astype(f32).reshape(PR, PC, chan)

        @pl.loop(0, TS // 8)
        def _(yb):
            y0 = yb * 8
            for lo, hi in ((0, 128), (128, chan)):
                acc = jnp.zeros((8, TS, hi - lo), f32)
                for k in range(KW):
                    shifted = padded[pl.ds(y0, 8 + KW - 1), k : k + TS, lo:hi]
                    for r in range(KW):
                        acc += taps_ref[r * KW + k : r * KW + k + 1, lo:hi][None] * shifted[r : r + 8]
                unit_s[pl.ds(y0, 8), :, lo:hi] = acc
            acc = unit_s[pl.ds(y0, 8)]
            mean = jnp.mean(acc, axis=2, keepdims=True)
            centred = acc - mean
            inv = lax.rsqrt(jnp.mean(centred * centred, axis=2, keepdims=True) + 1e-06)
            unit_s[pl.ds(y0, 8)] = centred * inv
            inv_s[pl.ds(y0, 8)] = jnp.broadcast_to(inv, (8, TS, 128))

        gain = gain_ref[...]
        unit = unit_s[...].reshape(CELLS, chan)
        feat = (unit * gain).astype(bf16)
        feats[pl.ds(a * CELLS, CELLS), :] = feat
        pre = jnp.dot(feat, win_ref[...], preferred_element_type=f32)
        keep = (lane_row < rows[a]).astype(f32)
        mgrad_t = (cot_ref[a].astype(f32) * keep).astype(bf16)
        grads_t[a] = mgrad_t
        mgrad = mgrad_t.astype(f32).T.astype(bf16)
        ghid = jnp.dot(mgrad, wout_ref[...], preferred_element_type=f32)
        square = pre * pre
        bend = jnp.tanh(0.7978845608028654 * pre * (1.0 + 0.044715 * square))
        half = 0.5 * (1.0 + bend)
        hidden = (pre * half).astype(bf16)
        slope = half + 0.5 * pre * (1.0 - bend * bend) * (0.7978845608028654 * (1.0 + 0.134145 * square))
        gpre = (ghid * slope).astype(bf16)
        hiddens[pl.ds(a * CELLS, CELLS), :] = hidden
        gpres[pl.ds(a * CELLS, CELLS), :] = gpre
        branch = lax.dot_general(
            hidden, wout_ref[...], (((1,), (1,)), ((), ())), preferred_element_type=f32
        )
        stem_own = padded[REACH : REACH + TS, REACH : REACH + TS, :].reshape(CELLS, chan)
        out_ref[a] = ((stem_own + branch).T * keep).astype(bf16)
        gfeat = lax.dot_general(gpre, win_ref[...], (((1,), (1,)), ((), ())), preferred_element_type=f32)
        gfeat = gfeat.astype(bf16).astype(f32)
        gacc[...] += jnp.sum((gfeat * unit).reshape(CELLS // 8, 8, chan), axis=0)
        scaled = gfeat * gain
        first = jnp.mean(scaled, axis=1, keepdims=True)
        second = jnp.mean(scaled * unit, axis=1, keepdims=True)
        inv = inv_s[...].reshape(CELLS, 128)[:, 0:1]
        gconv[...] = (inv * (scaled - first - unit * second)).reshape(TS, TS, chan)

        @pl.loop(0, TS // 8)
        def _(yb):
            y0 = yb * 8
            for lo, hi in ((0, 128), (128, chan)):
                grad = gconv[pl.ds(y0, 8), :, lo:hi]
                for k in range(KW):
                    shifted = padded[pl.ds(y0, 8 + KW - 1), k : k + TS, lo:hi]
                    for r in range(KW):
                        prod = grad * shifted[r : r + 8]
                        kacc[r * KW + k, :, lo:hi] += jnp.sum(prod.reshape(16, 8, hi - lo), axis=0)

    held[...] = jnp.zeros_like(held)
    small[...] = jnp.zeros_like(small)
    hid = win_ref.shape[1]
    held[0:chan, 0:hid] = lax.dot_general(
        feats[...], gpres[...], (((0,), (0,)), ((), ())), preferred_element_type=f32
    )
    total = jnp.zeros((chan, hid), f32)
    for a in range(tile_count):
        total += jnp.dot(grads_t[a], hiddens[a * CELLS : (a + 1) * CELLS, :], preferred_element_type=f32)
    held[0:chan, SIDE : SIDE + hid] = total
    small[0 : KW * KW, 0:chan] = jnp.sum(kacc[...], axis=1)
    small[KW * KW : KW * KW + 1, 0:chan] = jnp.sum(gacc[...], axis=0, keepdims=True)
    held[0:chan, hid:SIDE] = small[...].T[0:chan, 0 : SIDE - hid]
    for t in range(WIDE // 128):
        part = held[:, t * 128 : (t + 1) * 128].astype(bf16)
        pack_ref[t * ROWT : (t + 1) * ROWT] = part.reshape(ROWT, 16, 128)
    spare = pack_ref.shape[0] - USED
    pack_ref[USED:] = jnp.zeros((spare, 16, 128), bf16)


def unpack_kernel(total_ref, tiles_ref, gin_ref, gout_ref, gker_ref, ggain_ref, held):
    scale = 1.0 / total_ref[0]
    chan, hid = gin_ref.shape
    for t in range(WIDE // 128):
        part = tiles_ref[t * ROWT : (t + 1) * ROWT].astype(jnp.float32) * scale
        held[:, t * 128 : (t + 1) * 128] = part.reshape(ROWT * 16, 128)
    gin_ref[...] = held[0:chan, 0:hid]
    gout_ref[...] = held[0:chan, SIDE : SIDE + hid]
    base = SIDE - 128
    flipped = held[:, base:SIDE].T
    row = hid + KW * KW - base
    gker_ref[...] = flipped[hid - base : row, 0:chan]
    ggain_ref[...] = flipped[row : row + 1, 0:chan]


def greet(devices):
    barrier = pltpu.get_barrier_semaphore()
    for device in devices:
        pl.semaphore_signal(barrier, inc=1, device_id=device, device_id_type=pl.DeviceIdType.MESH)
    pl.semaphore_wait(barrier, len(devices))


def gather_kernel(with_lon, src, side, out, out_side, send_sem, recv_sem, own_sem):
    lat, lon = lax.axis_index("lat"), lax.axis_index("lon")
    z, x, core = lat // 4, (lat // 2) % 2, lat % 2

    def place(step):
        dz, dx, dc = step
        return ((z + dz) % 4) * 4 + ((x + dx) % 2) * 2 + (core + dc) % 2

    def device_of(step):
        return {"lat": place(step), "lon": lon}

    across = {"lat": lat, "lon": (lon + 1) % 2}
    peers = [device_of(p) for p in ((1, 0, 0), (2, 0, 0), (3, 0, 0), (0, 1, 0), (0, 0, 1))]
    greet(peers + [across] * with_lon)
    copies = {}

    def start(key, here, there, n, device):
        copy = pltpu.make_async_remote_copy(
            src_ref=here, dst_ref=there, send_sem=send_sem.at[n], recv_sem=recv_sem.at[n],
            device_id=device, device_id_type=pl.DeviceIdType.MESH,
        )
        copy.start()
        copies[key] = copy

    def send(which, block, hop, landed):
        target = out_side if which else out
        here = target.at[place(block)]
        if which == 0 and block == (0, 0, 0):
            here = src
        dz, dx, dc = landed
        n = which * 16 + (dz * 2 + dx) * 2 + dc
        start((which, landed), here, target.at[place(block)], n, device_of(hop))

    def forward(which, block):
        dz, dx, dc = block
        if dx == 0:
            send(which, block, (0, 1, 0), (dz, 1, 0))
        send(which, block, (0, 0, 1), (dz, dx, 1))

    def spread(which):
        for dz in (2, 1, 3):
            send(which, (0, 0, 0), (dz, 0, 0), ((4 - dz) % 4, 0, 0))
        forward(which, (0, 0, 0))

    if with_lon:
        start("side", side, out_side.at[lat], 32, across)
    spread(0)
    own = pltpu.make_async_copy(src, out.at[lat], own_sem)
    own.start()
    if with_lon:
        copies["side"].wait_recv()
        spread(1)
    kinds = (0, 1) if with_lon else (0,)
    for dz, dx in ((0, 1), (1, 0), (3, 0), (1, 1), (3, 1), (2, 0), (2, 1)):
        for which in kinds:
            copies[which, (dz, dx, 0)].wait_recv()
            forward(which, (dz, dx, 0))
    for which in kinds:
        for dz in range(4):
            for dx in range(2):
                copies[which, (dz, dx, 1)].wait_recv()
    for copy in copies.values():
        copy.wait_send()
    own.wait()


def reduce_kernel(n_lon, per, src, out, first, middle, second, acc, fourth, third, sems):
    lat, lon = lax.axis_index("lat"), lax.axis_index("lon")
    z, x, core = lat // 4, (lat // 2) % 2, lat % 2
    chips, deep = n_lon * 2, 4
    span = per * deep

    def chip(d):
        return (lon * 2 + x + d) % chips

    def device_at(d):
        q = chip(d)
        return {"lat": z * 4 + (q % 2) * 2 + core, "lon": q // 2}

    def along(d):
        other = (z + d) % deep
        return other, {"lat": other * 4 + lat % 4, "lon": lon}

    def region(d, half):
        return pl.ds((chip(d) * 2 + half) * span, span)

    partner = {"lat": z * 4 + x * 2 + 1 - core, "lon": lon}
    greet(
        [partner]
        + [device_at(d) for d in range(1, chips)]
        + [along(d)[1] for d in range(1, deep)]
    )
    copies = []

    def send(stage, back, here, there, device):
        copy = pltpu.make_async_remote_copy(
            src_ref=here, dst_ref=there, send_sem=sems.at[stage, 0, back], recv_sem=sems.at[stage, 1, back],
            device_id=device, device_id_type=pl.DeviceIdType.MESH,
        )
        copy.start()
        copies.append(copy)
        return copy

    f32, bf16 = jnp.float32, jnp.bfloat16
    order = list(range(1, chips)) + [0]
    halves = {}
    for d in order:
        halves[d] = send(0, d, src.at[region(d, 1 - core)], first.at[d], partner)
    landing = []
    for d in order:
        halves[d].wait_recv()
        pair = src[region(d, core)].astype(f32) + first[d].astype(f32)
        if d == 0:
            acc[...] = pair
        else:
            middle[d] = pair.astype(bf16)
            landing.append(send(1, chips - d, middle.at[d], second.at[chips - d], device_at(d)))
    for d in range(1, chips):
        landing[d - 1].wait_recv()
        acc[...] += second[chips - d].astype(f32)
    fourth[...] = acc[...].astype(bf16)
    landing = []
    for d in range(1, deep):
        other, device = along(d)
        landing.append(send(2, deep - d, fourth.at[pl.ds(other * per, per)], third.at[deep - d], device))
    total = acc[pl.ds(z * per, per)]
    for d in range(1, deep):
        landing[d - 1].wait_recv()
        total += third[deep - d].astype(f32)
    mark = pl.ds((chip(0) * 2 + core) * span + z * per, per)
    out[mark] = total.astype(bf16)
    landing = []
    for d in range(1, deep):
        landing.append(send(3, deep - d, out.at[mark], out.at[mark], along(d)[1]))
    for copy in landing:
        copy.wait_recv()
    whole = region(0, core)
    landing = []
    for d in range(1, chips):
        landing.append(send(4, chips - d, out.at[whole], out.at[whole], device_at(d)))
    final = [send(5, 0, out.at[whole], out.at[whole], partner)]
    for d in range(1, chips):
        landing[d - 1].wait_recv()
        came = region(chips - d, core)
        final.append(send(5, chips - d, out.at[came], out.at[came], partner))
    for copy in final:
        copy.wait_recv()
    for copy in copies:
        copy.wait_send()


def body(x_tiles, tile_pos, valid_rows, stem_w, dw_kernel, norm_gain, w_in, w_out, cotangent):
    f32 = jnp.float32
    bf16 = jnp.bfloat16
    lat_count = lax.axis_size("lat")
    lon_count = lax.axis_size("lon")
    inputs, places, rows, upstream = x_tiles[0], tile_pos[0], valid_rows[0], cotangent[0]
    tile_count, cin, _ = inputs.shape
    chan, hid = w_in.shape
    lanes = tile_count * EDGE
    smem = pl.BlockSpec(memory_space=pltpu.SMEM)
    vmem = pl.BlockSpec(memory_space=pltpu.VMEM)
    params = pltpu.CompilerParams(vmem_limit_bytes=VMEM_LIMIT)
    side_lanes = tile_count * SIDE_CELLS
    packed, packed_side = pl.pallas_call(
        pack_kernel,
        out_shape=[
            jax.ShapeDtypeStruct((CINP, lanes), bf16),
            jax.ShapeDtypeStruct((CINP, side_lanes), bf16),
        ],
        in_specs=[smem, smem, vmem, vmem, vmem],
        out_specs=[vmem, vmem],
        scratch_shapes=[pltpu.VMEM((CINP, lanes), f32), pltpu.VMEM((CINP, side_lanes), f32)],
        compiler_params=params,
    )(places, rows, inputs, jnp.asarray(edge_pick(), bf16), jnp.asarray(side_pick(), bf16))
    with_lon = lon_count == 2
    gathered, sides = pl.pallas_call(
        functools.partial(gather_kernel, with_lon),
        out_shape=[
            jax.ShapeDtypeStruct((lat_count, CINP, lanes), bf16),
            jax.ShapeDtypeStruct((lat_count, CINP, side_lanes), bf16),
        ],
        in_specs=[vmem, vmem],
        out_specs=[vmem, vmem],
        scratch_shapes=[
            pltpu.SemaphoreType.DMA((33,)),
            pltpu.SemaphoreType.DMA((33,)),
            pltpu.SemaphoreType.DMA,
        ],
        compiler_params=pltpu.CompilerParams(
            vmem_limit_bytes=VMEM_LIMIT, collective_id=0, has_side_effects=True
        ),
    )(packed, packed_side)
    if not with_lon:
        gathered = lax.all_gather(gathered, "lon", tiled=True)

    def described(blocks):
        meta = blocks[:, 77:80, 0:tile_count].astype(f32)
        return (meta[:, 0, :] * 16.0 + meta[:, 1, :]).astype(jnp.int32), jnp.sum(meta[:, 2, :])

    def found(want, keys):
        numbers = np.arange(keys.shape[0] * tile_count, dtype=np.int32)
        codes = jnp.asarray(numbers // tile_count * 8 + numbers % tile_count)
        hit = want[:, :, None] == keys.reshape(-1)[None, None, :]
        return 7 + jnp.sum(jnp.where(hit, codes - 7, 0), axis=2)

    off = np.array(OFFSETS, np.int32)
    want_row = (places >> 3)[:, None] + off[None, :, 0]
    want_col = (places & 7)[:, None] + off[None, :, 1]
    all_place, ocean_rows = described(gathered)
    if with_lon:
        side_place, side_rows = described(sides)
        cell_total = TS * (ocean_rows + side_rows)
        inside = (want_col >= 0) & (want_col < TCOLS)
        want = want_row * TCOLS + (want_col & 7)
        near = jnp.concatenate(
            [
                found(jnp.where(inside, want, -1), all_place),
                found(jnp.where(inside, -1, want), side_place),
            ],
            axis=1,
        )
    else:
        cell_total = TS * ocean_rows
        around = TCOLS * lon_count
        sector = jnp.arange(lon_count * lat_count, dtype=jnp.int32)[:, None] // lat_count
        keys = (all_place >> 3) * around + sector * TCOLS + (all_place & 7)
        want_col = (want_col + lax.axis_index("lon") * TCOLS) % around
        near = found(want_row * around + want_col, keys)
    pick = halo_pick(tile_count)
    groups = lon_count * 4
    per = -(-USED // (groups * 4))
    tiles_all = per * groups * 4
    result, packed_sums = pl.pallas_call(
        functools.partial(block_kernel, with_lon),
        out_shape=[
            jax.ShapeDtypeStruct((tile_count, chan, CELLS), bf16),
            jax.ShapeDtypeStruct((tiles_all, 16, 128), bf16),
        ],
        in_specs=[smem, smem] + [vmem] * 10,
        out_specs=[vmem] * 2,
        scratch_shapes=[
            pltpu.VMEM((ROWT * 16, WIDE), f32),
            pltpu.VMEM((128, 256), f32),
            pltpu.VMEM((CINP, chan), bf16),
            pltpu.VMEM((tile_count, CINP, pick.shape[0]), bf16),
            pltpu.VMEM((tile_count, CINP, PR * PC), f32),
            pltpu.VMEM((PR, PC, chan), f32),
            pltpu.VMEM((TS, TS, chan), f32),
            pltpu.VMEM((TS, TS, 128), f32),
            pltpu.VMEM((tile_count * CELLS, chan), bf16),
            pltpu.VMEM((tile_count * CELLS, hid), bf16),
            pltpu.VMEM((tile_count * CELLS, hid), bf16),
            pltpu.VMEM((tile_count, chan, CELLS), bf16),
            pltpu.VMEM((TS, TS, chan), f32),
            pltpu.VMEM((KW * KW, 8, chan), f32),
            pltpu.VMEM((8, chan), f32),
        ],
        compiler_params=params,
    )(
        near, rows, gathered, sides, inputs, upstream, jnp.asarray(pick, bf16),
        stem_w, dw_kernel.T, norm_gain[None], w_in, w_out.T,
    )
    span = per * 4
    chips = lon_count * 2
    reduced = pl.pallas_call(
        functools.partial(reduce_kernel, lon_count, per),
        out_shape=jax.ShapeDtypeStruct((tiles_all, 16, 128), bf16),
        in_specs=[vmem],
        out_specs=vmem,
        scratch_shapes=[
            pltpu.VMEM((chips, span, 16, 128), bf16),
            pltpu.VMEM((chips, span, 16, 128), bf16),
            pltpu.VMEM((chips, span, 16, 128), bf16),
            pltpu.VMEM((span, 16, 128), f32),
            pltpu.VMEM((span, 16, 128), bf16),
            pltpu.VMEM((4, per, 16, 128), bf16),
            pltpu.SemaphoreType.DMA((6, 2, max(chips, 4))),
        ],
        compiler_params=pltpu.CompilerParams(
            vmem_limit_bytes=VMEM_LIMIT, collective_id=1, has_side_effects=True
        ),
    )(packed_sums)
    sum_in, sum_out, sum_kernel, sum_gain = pl.pallas_call(
        unpack_kernel,
        out_shape=[
            jax.ShapeDtypeStruct((chan, hid), f32),
            jax.ShapeDtypeStruct((chan, hid), f32),
            jax.ShapeDtypeStruct((KW * KW, chan), f32),
            jax.ShapeDtypeStruct((1, chan), f32),
        ],
        in_specs=[smem, vmem],
        out_specs=[vmem] * 4,
        scratch_shapes=[pltpu.VMEM((ROWT * 16, WIDE), f32)],
        compiler_params=params,
    )(cell_total.reshape(1), reduced)
    return result[None], sum_in, sum_out.T, sum_kernel.T, sum_gain[0]


def solution(mesh):
    in_specs = (
        P("lon", "lat", None, None),
        P("lon", "lat"),
        P("lon", "lat"),
        P(),
        P(),
        P(),
        P(),
        P(),
        P("lon", "lat", None, None),
    )
    out_specs = (P("lon", "lat", None, None), P(), P(), P(), P())
    return jax.shard_map(body, mesh=mesh, in_specs=in_specs, out_specs=out_specs, check_vma=False)
```
